32 devices in a mesh: grp: 2 (over x), row: 4 (over y, core), col: 4 (over z).
Axes of the slice: x: 2, y: 2, z: 4, core: 2. Of those that a mesh axis runs over, the one named last changes fastest.
Arguments:
- amplitudes: bfloat16 [64, 4, 256, 256], P(('grp', 'row'), 'col'), may hold values from -6 to 6
- factors: bfloat16 [4, 256, 256], P('col'), may hold values from -0.1875 to 0.1875
- cycle_weight: bfloat16 [16384, 16384], P('col', 'row'), may hold values from -0.046875 to 0.046875
- orbital_order: int32 [256], replicated, may hold values from 0 to 255, each once
Outputs:
- ladder_term: bfloat16 [64, 4, 256, 256], P(('grp', 'row'), 'col')
- cycle_term: bfloat16 [1024, 16384], P(('grp', 'row'), 'col')
The draws below stay inside these ranges and needn't reach their ends.
Inputs may be any that keep to these rules, and one draw needn't show every extreme that they name: `orbital_order`: each of 0 to 255 appears exactly once.
All inputs are finite; a program needn't handle non-finite values.
Results may differ from the reference program's by a relative error of at most 0.0049.
Values may be sent and summed in bfloat16 or wider, within the bound.
A program may use at most 128 MiB of HBM per device.

```python
import jax
import jax.numpy as jnp
from jax import lax

OCC = 64
VIRT = 256
NAUX = 4
JW = 4
NPH = 16384
PANELS = 2
PANEL_V = 128
COLS = 1024


def level_of(own_key, extent, split, smallest, top_value):
    def one(position, blocks):
        steps = jax.random.uniform(jax.random.fold_in(jax.random.fold_in(own_key, 6), position), (blocks,), jnp.float32, smallest / len(split), top_value / len(split))
        return jnp.repeat(jnp.exp(steps), extent[position] // blocks).reshape((-1,) + (1,) * (len(extent) - position - 1))

    level = one(*split[0])
    for cut in split[1:]:
        level = level * one(*cut)
    return level


def bell_draw(key, shape, spread, limit, shards=(), held_as=jnp.bfloat16):
    loudness = level_of(key, shape, shards, -0.22, 0.18) if shards else 1.0
    array = jax.random.normal(key, shape, jnp.float32) * spread * loudness
    return jnp.minimum(jnp.maximum(array, -limit), limit).astype(held_as)


def setup_inputs(seed: int = 0) -> dict:
    splits = jax.random.split(jax.random.key(seed), 5)
    amplitudes = bell_draw(splits[0], (OCC, JW, VIRT, VIRT), 1.0, 6.0, ((0, 8), (1, 4)))
    factors = bell_draw(splits[1], (NAUX, VIRT, VIRT), (VIRT * 4) ** -0.5, 0.1875, ((0, 4),))
    cycle_weight = bell_draw(splits[2], (NPH, NPH), NPH ** -0.5, 0.046875, ((0, 4), (1, 4)))
    orbital_order = jax.random.permutation(splits[3], VIRT).astype(jnp.int32)
    return {"amplitudes": amplitudes, "factors": factors, "cycle_weight": cycle_weight, "orbital_order": orbital_order}


def reference(amplitudes, factors, cycle_weight, orbital_order):
    pairs_wide = amplitudes.astype(jnp.float32)

    def add_factor(running, factor):
        factor_wide = factor.astype(jnp.float32)
        dressed = jnp.einsum("ac,kjcd->kjad", factor_wide, pairs_wide, precision=lax.Precision.HIGHEST)
        dressed = lax.optimization_barrier(dressed.astype(jnp.bfloat16)).astype(jnp.float32)
        update = jnp.einsum("kjad,bd->kjab", dressed, factor_wide, precision=lax.Precision.HIGHEST)
        return running + update, None

    zero_sum = jnp.zeros((OCC, JW, VIRT, VIRT), jnp.float32)
    ladder_sum, unused = lax.scan(add_factor, zero_sum, factors)
    ordered = jnp.take(amplitudes, orbital_order, axis=3)
    ordered = ordered.reshape(OCC, JW, VIRT, PANELS, PANEL_V)
    panel = jnp.transpose(ordered, (2, 0, 3, 1, 4)).reshape(NPH, COLS)
    cycle_sum = jnp.dot(cycle_weight.astype(jnp.float32), panel.astype(jnp.float32), precision=lax.Precision.HIGHEST)
    return ladder_sum.astype(jnp.bfloat16), cycle_sum.T.astype(jnp.bfloat16)
```

```python
import functools

import jax
import jax.numpy as jnp
from jax import lax
from jax.experimental import pallas as pl
from jax.experimental.pallas import tpu as pltpu
from jax.sharding import PartitionSpec as P

MESH = pl.DeviceIdType.MESH
TILE = 16
LANES = 128
PARTS = 4
NT = (((1,), (1,)), ((), ()))


def dress_pairs(factor_piece, pair_stack):
    dressed = jnp.einsum(
        "pac,qcd->pqad", factor_piece, pair_stack, preferred_element_type=jnp.float32
    ).astype(jnp.bfloat16)
    return jnp.einsum("pqad,pbd->qab", dressed, factor_piece, preferred_element_type=jnp.float32)


def plain_shards(amplitudes, factors, cycle_weight, orbital_order):
    occ_rows = amplitudes.shape[0]
    occ_cols = amplitudes.shape[1]
    virtual = amplitudes.shape[2]
    pair_stack = amplitudes.reshape(occ_rows * occ_cols, virtual, virtual)
    ladder_sum = dress_pairs(lax.all_gather(factors, "col", axis=0, tiled=True), pair_stack)
    ladder_sum = ladder_sum.reshape(occ_rows, occ_cols, virtual, virtual)
    ladder_term = ladder_sum.astype(jnp.bfloat16)
    groups = lax.axis_size("grp")
    row_count = lax.axis_size("row")
    panel_width = virtual // groups
    block_width = virtual // row_count
    ordered = jnp.take(amplitudes, orbital_order, axis=3)
    ordered = ordered.reshape(occ_rows, occ_cols, row_count, block_width, groups, panel_width)
    outgoing = jnp.transpose(ordered, (4, 2, 3, 0, 1, 5))
    outgoing = outgoing.reshape(groups * row_count, block_width, 1, occ_rows, occ_cols, panel_width)
    arrived = lax.all_to_all(outgoing, ("grp", "row"), split_axis=0, concat_axis=2, tiled=True)
    column_tile = arrived.reshape(
        block_width * groups * row_count * occ_rows, occ_cols * panel_width
    )
    products = lax.dot_general(
        lax.all_gather(column_tile, "col", axis=1, tiled=True),
        cycle_weight,
        (((0,), (1,)), ((), ())),
        preferred_element_type=jnp.float32,
    )
    cycle_term = lax.psum_scatter(products, "row", scatter_dimension=0, tiled=True).astype(
        jnp.bfloat16
    )
    return (ladder_term, cycle_term)


def kernel(
    sizes, order_ref, amp, fac, weight, ladder_out, cycle_out,
    wv, own, other, staged, panel, acc, pair_out, pair_in, far_out, far_in, result, fitted,
    load_sem, weight_sem, raw_send, raw_recv, ex_send, ex_recv, up_send, down_send, z_recv,
    fit_send, fit_recv, fan_send, fan_recv, pair_send, pair_recv, far_send, far_recv, out_sem,
):
    groups, rows, cols = sizes
    sides = rows // 2
    chips = groups * sides
    pairs, virtual, _ = amp.shape
    block = virtual // rows
    chunks = block // TILE
    depth = weight.shape[1] // chunks
    span = weight.shape[0] // PARTS
    panel_width = virtual // groups
    g, r, z = lax.axis_index("grp"), lax.axis_index("row"), lax.axis_index("col")
    side, core = r // 2, r % 2
    mate = side * 2 + 1 - core
    chip = g * sides + side
    place = g * rows + r
    fit_rows = virtual // (groups * rows)

    def at(gg, rr, zz):
        return {"grp": gg, "row": rr, "col": zz}

    def remote(src, dst, send, recv, where):
        return pltpu.make_async_remote_copy(
            src_ref=src, dst_ref=dst, send_sem=send, recv_sem=recv,
            device_id=where, device_id_type=MESH,
        )

    mine = pl.ds(pl.multiple_of(place * fit_rows, fit_rows), fit_rows)
    load_own = pltpu.make_async_copy(amp, own, load_sem.at[0])
    load_own.start()
    load_fit = pltpu.make_async_copy(fac.at[0, mine], fitted.at[z, mine], load_sem.at[1])
    load_fit.start()

    def load_weight(c):
        return pltpu.make_async_copy(
            weight.at[:, pl.ds(c * depth, depth)], wv.at[c], weight_sem.at[c]
        )

    for c in range(chunks):
        load_weight(c).start()

    peers = groups * rows - 1
    barrier = pltpu.get_barrier_semaphore()
    for step in range(1, peers + 1):
        q = lax.rem(place + step, groups * rows)
        pl.semaphore_signal(barrier, inc=1, device_id=at(q // rows, q % rows, z), device_id_type=MESH)
    for step in range(1, cols):
        pl.semaphore_signal(
            barrier, inc=1, device_id=at(g, r, lax.rem(z + step, cols)), device_id_type=MESH
        )
    pl.semaphore_wait(barrier, peers + cols - 1)

    def raw_copy(s):
        first = pl.multiple_of((s * 2 + 1 - core) * block, block)
        return remote(
            amp.at[:, pl.ds(first, block)], other.at[s], raw_send.at[s], raw_recv.at[s],
            at(g, mate, z),
        )

    for s in range(sides):
        raw_copy(s).start()

    load_fit.wait()

    def fit_copy(step):
        here = fitted.at[z, mine]
        return remote(
            here, here, fit_send.at[step - 1], fit_recv.at[step - 1],
            at(g, r, lax.rem(z + step, cols)),
        )

    for step in range(1, cols):
        fit_copy(step).start()

    load_own.wait()

    width = 2 * pairs * TILE
    pick = (
        lax.broadcasted_iota(jnp.int32, (virtual, virtual), 0) == order_ref[...]
    ).astype(jnp.float32).astype(jnp.bfloat16)
    to_row = lax.broadcasted_iota(jnp.int32, (width, width), 0)
    from_row = lax.broadcasted_iota(jnp.int32, (width, width), 1)
    k_row = to_row & (2 * pairs - 1)
    c_row = to_row // (2 * pairs)
    late = (k_row // pairs) ^ core
    turn = (
        from_row == late * (pairs * TILE) + (k_row & (pairs - 1)) * TILE + c_row
    ).astype(jnp.float32).astype(jnp.bfloat16)

    slot = pl.ds(pl.multiple_of(chip * TILE, TILE), TILE)

    def ex_copy(c, s, q):
        return remote(
            staged.at[c, s, q], panel.at[z, c, :, slot, :],
            ex_send.at[c, s * groups + q], ex_recv.at[c, chip], at(q, s * 2 + core, z),
        )

    for s in range(sides):
        raw_copy(s).wait_recv()

    def exchange(c, carry):
        for s in range(sides):
            first = pl.multiple_of((s * 2 + core) * block + c * TILE, TILE)
            near = own[:, pl.ds(first, TILE), :].reshape(pairs * TILE, virtual)
            far = other[s, :, pl.ds(pl.multiple_of(c * TILE, TILE), TILE), :].reshape(
                pairs * TILE, virtual
            )
            both = jnp.concatenate([near, far], axis=0)
            picked = jnp.dot(both, pick, preferred_element_type=jnp.float32).astype(jnp.bfloat16)
            turned = jnp.dot(turn, picked, preferred_element_type=jnp.float32).astype(jnp.bfloat16)
            for q in range(groups):
                part = turned[:, q * panel_width:(q + 1) * panel_width]
                part = part.reshape(TILE, 2 * pairs, panel_width)
                here = (q == g) & (s == side)

                @pl.when(here)
                def _():
                    panel[z, c, :, slot, :] = part

                @pl.when(jnp.logical_not(here))
                def _():
                    staged[c, s, q] = part
                    ex_copy(c, s, q).start()
        return carry

    lax.fori_loop(0, chunks, exchange, 0)

    def up_copy(j, c):
        piece = panel.at[j, c]
        return remote(piece, piece, up_send.at[j, c], z_recv.at[j, c], at(g, r, z + 1))

    def down_copy(j, c):
        piece = panel.at[j, c]
        return remote(piece, piece, down_send.at[j, c], z_recv.at[j, c], at(g, r, z - 1))

    def multiply(j, c, first):
        piece = panel[j, c].reshape(depth, panel_width)

        def one(i, carry):
            sl = pl.ds(pl.multiple_of(i * span, span), span)
            product = jnp.dot(wv[c, sl, :], piece, preferred_element_type=jnp.float32)
            if first:
                @pl.when(c == 0)
                def _():
                    acc[j, sl, :] = product

                @pl.when(c > 0)
                def _():
                    acc[j, sl, :] += product
            else:
                acc[j, sl, :] = jnp.where(c == 0, product, acc[j, sl, :] + product)
            return carry

        lax.fori_loop(0, PARTS, one, 0)

    def pair_copy(j, i):
        sl = pl.ds(pl.multiple_of(i * span, span), span)
        h = j // 2
        return remote(
            pair_out.at[h, sl], pair_in.at[h, sl], pair_send.at[h, i], pair_recv.at[h, i],
            at(g, mate, z),
        )

    def far_copy(i):
        sl = pl.ds(pl.multiple_of(i * span, span), span)
        return remote(
            far_out.at[sl], far_in.at[sl], far_send.at[i], far_recv.at[i],
            at(g, (1 - side) * 2 + core, z),
        )

    def give(j):
        @pl.when(j % 2 != core)
        def _():
            def one(i, carry):
                sl = pl.ds(pl.multiple_of(i * span, span), span)
                pair_out[j // 2, sl, :] = acc[j, sl, :].astype(jnp.bfloat16)
                pair_copy(j, i).start()
                return carry

            lax.fori_loop(0, PARTS, one, 0)

    def pass_on(j):
        @pl.when((j % 2 == core) & (j // 2 != side))
        def _():
            def one(i, carry):
                sl = pl.ds(pl.multiple_of(i * span, span), span)
                pair_copy(j, i).wait_recv()
                total = acc[j, sl, :] + pair_in[j // 2, sl, :].astype(jnp.float32)
                far_out[sl, :] = total.astype(jnp.bfloat16)
                far_copy(i).start()
                return carry

            lax.fori_loop(0, PARTS, one, 0)

    def first_hop(c, carry):
        for q in range(chips):
            @pl.when(q != chip)
            def _():
                landing = panel.at[z, c, :, pl.ds(q * TILE, TILE), :]
                remote(
                    landing, landing, ex_send.at[c, 0], ex_recv.at[c, q], at(g, mate, z)
                ).wait_recv()

        @pl.when(z + 1 < cols)
        def _():
            up_copy(z, c).start()

        @pl.when(z > 0)
        def _():
            down_copy(z, c).start()

        load_weight(c).wait()
        multiply(z, c, True)
        return carry

    lax.fori_loop(0, chunks, first_hop, 0)

    def fan_copy(step):
        q = lax.rem(place + step, groups * rows)
        here = fitted.at[:, mine]
        return remote(
            here, here, fan_send.at[step - 1], fan_recv.at[step - 1], at(q // rows, q % rows, z)
        )

    for step in range(1, cols):
        fit_copy(step).wait_recv()
    for step in range(1, peers + 1):
        fan_copy(step).start()
    give(z)
    pass_on(z)

    def ladder(k):
        left = own[k]
        total = jnp.zeros((virtual, virtual), jnp.float32)
        for p in range(cols):
            dressed = jnp.dot(fitted[p], left, preferred_element_type=jnp.float32)
            total += lax.dot_general(
                dressed.astype(jnp.bfloat16), fitted[p], NT, preferred_element_type=jnp.float32
            )
        own[k] = total.astype(jnp.bfloat16)

    def hop(n, carry):
        low, high = z - n, z + n

        def step(c, inner):
            @pl.when(low >= 0)
            def _():
                up_copy(low, c).wait_recv()

                @pl.when(z + 1 < cols)
                def _():
                    up_copy(low, c).start()

            @pl.when(high < cols)
            def _():
                down_copy(high, c).wait_recv()

                @pl.when(z > 0)
                def _():
                    down_copy(high, c).start()

            @pl.when(low >= 0)
            def _():
                multiply(low, c, True)

            @pl.when(high < cols)
            def _():
                multiply(high, c, True)

            return inner

        lax.fori_loop(0, chunks, step, 0)
        for j, valid in ((low, low >= 0), (high, high < cols)):
            @pl.when(valid)
            def _():
                give(j)
        for j, valid in ((low, low >= 0), (high, high < cols)):
            @pl.when(valid)
            def _():
                pass_on(j)

        @pl.when(n == 1)
        def _():
            for step in range(1, peers + 1):
                fan_copy(step).wait_recv()

            def one(k, inner):
                ladder(k)
                return inner

            lax.fori_loop(0, pairs, one, 0)
            pltpu.make_async_copy(own, ladder_out, load_sem.at[0]).start()

        return carry

    lax.fori_loop(1, cols, hop, 0)

    def out_copy(i):
        return pltpu.make_async_copy(
            result.at[i], cycle_out.at[:, pl.ds(i * span, span)], out_sem.at[i]
        )

    for i in range(PARTS):
        sl = pl.ds(i * span, span)
        pair_copy(r, i).wait_recv()
        far_copy(i).wait_recv()
        total = acc[r, sl, :] + pair_in[side, sl, :].astype(jnp.float32)
        total += far_in[sl, :].astype(jnp.float32)
        result[i] = total.T.astype(jnp.bfloat16)
        out_copy(i).start()

    pltpu.make_async_copy(own, ladder_out, load_sem.at[0]).wait()
    for s in range(sides):
        raw_copy(s).wait_send()
    for step in range(1, cols):
        fit_copy(step).wait_send()
    for step in range(1, peers + 1):
        fan_copy(step).wait_send()

    def drain(c, carry):
        for s in range(sides):
            for q in range(groups):
                @pl.when(jnp.logical_not((q == g) & (s == side)))
                def _():
                    ex_copy(c, s, q).wait_send()
        for j in range(cols):
            @pl.when((j <= z) & (z + 1 < cols))
            def _():
                up_copy(j, c).wait_send()

            @pl.when((j >= z) & (z > 0))
            def _():
                down_copy(j, c).wait_send()
        return carry

    lax.fori_loop(0, chunks, drain, 0)
    for i in range(PARTS):
        for h in range(sides):
            pair_copy(2 * h, i).wait_send()
        far_copy(i).wait_send()
        out_copy(i).wait()


def fused_shards(sizes, amplitudes, factors, cycle_weight, orbital_order):
    groups, rows, cols = sizes
    pairs, one, virtual, _ = amplitudes.shape
    out_width, depth = cycle_weight.shape
    block = virtual // rows
    chunks = block // TILE
    chips = groups * rows // 2
    panel_width = virtual // groups
    span = out_width // PARTS
    half = jnp.bfloat16
    dma = pltpu.SemaphoreType.DMA
    anywhere = pl.BlockSpec(memory_space=pl.ANY)
    matmuls = 2 * out_width * depth * cols * panel_width
    ladder_term, cycle_term = pl.pallas_call(
        functools.partial(kernel, sizes),
        out_shape=(
            jax.ShapeDtypeStruct((pairs, virtual, virtual), half),
            jax.ShapeDtypeStruct((panel_width, out_width), half),
        ),
        in_specs=[pl.BlockSpec(memory_space=pltpu.VMEM), anywhere, anywhere, anywhere],
        out_specs=(anywhere, anywhere),
        scratch_shapes=[
            pltpu.VMEM((chunks, out_width, depth // chunks), half),
            pltpu.VMEM((pairs, virtual, virtual), half),
            pltpu.VMEM((rows // 2, pairs, block, virtual), half),
            pltpu.VMEM((chunks, rows // 2, groups, TILE, 2 * pairs, panel_width), half),
            pltpu.VMEM((cols, chunks, TILE, 2 * pairs * chips, panel_width), half),
            pltpu.VMEM((cols, out_width, panel_width), jnp.float32),
            pltpu.VMEM((rows // 2, out_width, panel_width), half),
            pltpu.VMEM((rows // 2, out_width, panel_width), half),
            pltpu.VMEM((out_width, panel_width), half),
            pltpu.VMEM((out_width, panel_width), half),
            pltpu.VMEM((PARTS, panel_width, span), half),
            pltpu.VMEM((cols, virtual, virtual), half),
            dma((2,)),
            dma((chunks,)),
            dma((rows // 2,)),
            dma((rows // 2,)),
            dma((chunks, chips)),
            dma((chunks, chips)),
            dma((cols, chunks)),
            dma((cols, chunks)),
            dma((cols, chunks)),
            dma((cols - 1,)),
            dma((cols - 1,)),
            dma((groups * rows - 1,)),
            dma((groups * rows - 1,)),
            dma((rows // 2, PARTS)),
            dma((rows // 2, PARTS)),
            dma((PARTS,)),
            dma((PARTS,)),
            dma((PARTS,)),
        ],
        compiler_params=pltpu.CompilerParams(
            collective_id=0, has_side_effects=True, vmem_limit_bytes=60 * 1024 * 1024
        ),
        cost_estimate=pl.CostEstimate(
            flops=matmuls, bytes_accessed=2 * out_width * depth, transcendentals=0
        ),
    )(
        orbital_order.reshape(1, virtual),
        amplitudes.reshape(pairs, virtual, virtual),
        factors,
        cycle_weight,
    )
    return ladder_term.reshape(pairs, one, virtual, virtual), cycle_term


def shards(amplitudes, factors, cycle_weight, orbital_order):
    groups, rows, cols = (lax.axis_size(name) for name in ("grp", "row", "col"))
    pairs, per_col, virtual, _ = amplitudes.shape
    out_width, depth = cycle_weight.shape
    fits = (
        per_col == 1
        and factors.shape[0] == 1
        and rows == cols
        and rows // 2 == 2
        and rows % 2 == 0
        and 2 * pairs == TILE
        and virtual == groups * LANES
        and virtual % (rows * TILE) == 0
        and virtual % (groups * rows * TILE) == 0
        and depth == virtual // rows * groups * rows * pairs
        and out_width % (PARTS * LANES) == 0
        and 2 * out_width * depth <= 36 * 1024 * 1024
    )
    if fits:
        return fused_shards((groups, rows, cols), amplitudes, factors, cycle_weight, orbital_order)
    return plain_shards(amplitudes, factors, cycle_weight, orbital_order)


def solution(mesh):
    return jax.shard_map(
        shards,
        mesh=mesh,
        in_specs=(P(("grp", "row"), "col", None, None), P("col", None, None), P("col", "row"), P()),
        out_specs=(P(("grp", "row"), "col", None, None), P(("grp", "row"), "col")),
        check_vma=False,
    )
```

```python
import functools

import jax
import jax.numpy as jnp
from jax import lax
from jax.experimental import pallas as pl
from jax.experimental.pallas import tpu as pltpu
from jax.sharding import PartitionSpec as P

MESH = pl.DeviceIdType.MESH
TILE = 16
LANES = 128
PARTS = 4
NT = (((1,), (1,)), ((), ()))


def dress_pairs(factor_piece, pair_stack):
    dressed = jnp.einsum(
        "pac,qcd->pqad", factor_piece, pair_stack, preferred_element_type=jnp.float32
    ).astype(jnp.bfloat16)
    return jnp.einsum("pqad,pbd->qab", dressed, factor_piece, preferred_element_type=jnp.float32)


def plain_shards(amplitudes, factors, cycle_weight, orbital_order):
    occ_rows = amplitudes.shape[0]
    occ_cols = amplitudes.shape[1]
    virtual = amplitudes.shape[2]
    pair_stack = amplitudes.reshape(occ_rows * occ_cols, virtual, virtual)
    ladder_sum = dress_pairs(lax.all_gather(factors, "col", axis=0, tiled=True), pair_stack)
    ladder_sum = ladder_sum.reshape(occ_rows, occ_cols, virtual, virtual)
    ladder_term = ladder_sum.astype(jnp.bfloat16)
    groups = lax.axis_size("grp")
    row_count = lax.axis_size("row")
    panel_width = virtual // groups
    block_width = virtual // row_count
    ordered = jnp.take(amplitudes, orbital_order, axis=3)
    ordered = ordered.reshape(occ_rows, occ_cols, row_count, block_width, groups, panel_width)
    outgoing = jnp.transpose(ordered, (4, 2, 3, 0, 1, 5))
    outgoing = outgoing.reshape(groups * row_count, block_width, 1, occ_rows, occ_cols, panel_width)
    arrived = lax.all_to_all(outgoing, ("grp", "row"), split_axis=0, concat_axis=2, tiled=True)
    column_tile = arrived.reshape(
        block_width * groups * row_count * occ_rows, occ_cols * panel_width
    )
    products = lax.dot_general(
        lax.all_gather(column_tile, "col", axis=1, tiled=True),
        cycle_weight,
        (((0,), (1,)), ((), ())),
        preferred_element_type=jnp.float32,
    )
    cycle_term = lax.psum_scatter(products, "row", scatter_dimension=0, tiled=True).astype(
        jnp.bfloat16
    )
    return (ladder_term, cycle_term)


def kernel(
    sizes, order_ref, amp, fac, weight, ladder_out, cycle_out,
    wv, own, other, staged, panel, acc, pair_out, pair_in, far_out, far_in, result, fitted,
    load_sem, weight_sem, raw_send, raw_recv, ex_send, ex_recv, up_send, down_send, z_recv,
    fit_send, fit_recv, fan_send, fan_recv, pair_send, pair_recv, far_send, far_recv, out_sem,
):
    groups, rows, cols = sizes
    sides = rows // 2
    chips = groups * sides
    pairs, virtual, _ = amp.shape
    block = virtual // rows
    chunks = block // TILE
    depth = weight.shape[1] // chunks
    span = weight.shape[0] // PARTS
    panel_width = virtual // groups
    g, r, z = lax.axis_index("grp"), lax.axis_index("row"), lax.axis_index("col")
    side, core = r // 2, r % 2
    mate = side * 2 + 1 - core
    chip = g * sides + side
    place = g * rows + r
    fit_rows = virtual // (groups * rows)

    def at(gg, rr, zz):
        return {"grp": gg, "row": rr, "col": zz}

    def remote(src, dst, send, recv, where):
        return pltpu.make_async_remote_copy(
            src_ref=src, dst_ref=dst, send_sem=send, recv_sem=recv,
            device_id=where, device_id_type=MESH,
        )

    mine = pl.ds(pl.multiple_of(place * fit_rows, fit_rows), fit_rows)
    load_own = pltpu.make_async_copy(amp, own, load_sem.at[0])
    load_own.start()
    load_fit = pltpu.make_async_copy(fac.at[0, mine], fitted.at[z, mine], load_sem.at[1])
    load_fit.start()

    def load_weight(c):
        return pltpu.make_async_copy(
            weight.at[:, pl.ds(c * depth, depth)], wv.at[c], weight_sem.at[c]
        )

    for c in range(chunks):
        load_weight(c).start()

    peers = groups * rows - 1
    barrier = pltpu.get_barrier_semaphore()
    for step in range(1, peers + 1):
        q = lax.rem(place + step, groups * rows)
        pl.semaphore_signal(barrier, inc=1, device_id=at(q // rows, q % rows, z), device_id_type=MESH)
    for step in range(1, cols):
        pl.semaphore_signal(
            barrier, inc=1, device_id=at(g, r, lax.rem(z + step, cols)), device_id_type=MESH
        )
    pl.semaphore_wait(barrier, peers + cols - 1)

    def raw_copy(c, s):
        first = pl.multiple_of((s * 2 + 1 - core) * block + c * TILE, TILE)
        return remote(
            amp.at[:, pl.ds(first, TILE)], other.at[c, s], raw_send.at[c, s], raw_recv.at[c, s],
            at(g, mate, z),
        )

    for c in range(chunks):
        for s in range(sides):
            raw_copy(c, s).start()

    load_fit.wait()

    def fit_copy(step):
        here = fitted.at[z, mine]
        return remote(
            here, here, fit_send.at[step - 1], fit_recv.at[step - 1],
            at(g, r, lax.rem(z + step, cols)),
        )

    for step in range(1, cols):
        fit_copy(step).start()

    load_own.wait()

    width = 2 * pairs * TILE
    pick = (
        lax.broadcasted_iota(jnp.int32, (virtual, virtual), 0) == order_ref[...]
    ).astype(jnp.float32).astype(jnp.bfloat16)
    to_row = lax.broadcasted_iota(jnp.int32, (width, width), 0)
    from_row = lax.broadcasted_iota(jnp.int32, (width, width), 1)
    k_row = to_row & (2 * pairs - 1)
    c_row = to_row // (2 * pairs)
    late = (k_row // pairs) ^ core
    turn = (
        from_row == late * (pairs * TILE) + (k_row & (pairs - 1)) * TILE + c_row
    ).astype(jnp.float32).astype(jnp.bfloat16)

    slot = pl.ds(pl.multiple_of(chip * TILE, TILE), TILE)

    def ex_copy(c, s, q):
        return remote(
            staged.at[c, s, q], panel.at[z, c, :, slot, :],
            ex_send.at[c, s * groups + q], ex_recv.at[c, chip], at(q, s * 2 + core, z),
        )

    end_plane = (z == 0) | (z == cols - 1)
    late_block = jnp.where(z == 0, 1, cols - 2)
    late_in = end_plane & (late_block // 2 == side)
    late_up = (z == cols - 2) & ((cols - 2) // 2 == side)
    late_down = (z == 1) & (1 // 2 == side)
    half = chunks // 2

    def up_copy(j, c):
        piece = panel.at[j, c]
        return remote(piece, piece, up_send.at[j, c], z_recv.at[j, c], at(g, r, z + 1))

    def down_copy(j, c):
        piece = panel.at[j, c]
        return remote(piece, piece, down_send.at[j, c], z_recv.at[j, c], at(g, r, z - 1))

    def send_own(c):
        for q in range(chips):
            @pl.when(q != chip)
            def _():
                landing = panel.at[z, c, :, pl.ds(q * TILE, TILE), :]
                remote(
                    landing, landing, ex_send.at[c, 0], ex_recv.at[c, q], at(g, mate, z)
                ).wait_recv()

        @pl.when((z + 1 < cols) & jnp.logical_not(late_up & (c >= half)))
        def _():
            up_copy(z, c).start()

        @pl.when((z > 0) & jnp.logical_not(late_down & (c >= half)))
        def _():
            down_copy(z, c).start()

    def exchange(c, carry):
        for s in range(sides):
            raw_copy(c, s).wait_recv()
        for s in range(sides):
            first = pl.multiple_of((s * 2 + core) * block + c * TILE, TILE)
            near = own[:, pl.ds(first, TILE), :].reshape(pairs * TILE, virtual)
            far = other[c, s].reshape(pairs * TILE, virtual)
            both = jnp.concatenate([near, far], axis=0)
            picked = jnp.dot(both, pick, preferred_element_type=jnp.float32).astype(jnp.bfloat16)
            turned = jnp.dot(turn, picked, preferred_element_type=jnp.float32).astype(jnp.bfloat16)
            for q in range(groups):
                part = turned[:, q * panel_width:(q + 1) * panel_width]
                part = part.reshape(TILE, 2 * pairs, panel_width)
                here = (q == g) & (s == side)

                @pl.when(here)
                def _():
                    panel[z, c, :, slot, :] = part

                @pl.when(jnp.logical_not(here))
                def _():
                    staged[c, s, q] = part
                    ex_copy(c, s, q).start()

        @pl.when(c > 0)
        def _():
            send_own(c - 1)

        return carry

    lax.fori_loop(0, chunks, exchange, 0)
    send_own(chunks - 1)

    def multiply(j, c):
        piece = panel[j, c].reshape(depth, panel_width)

        def one(i, carry):
            sl = pl.ds(pl.multiple_of(i * span, span), span)
            product = jnp.dot(wv[c, sl, :], piece, preferred_element_type=jnp.float32)

            @pl.when(c == 0)
            def _():
                acc[j, sl, :] = product

            @pl.when(c > 0)
            def _():
                acc[j, sl, :] += product

            @pl.when((c == chunks - 1) & (j % 2 != core))
            def _():
                pair_out[j // 2, sl, :] = acc[j, sl, :].astype(jnp.bfloat16)
                pair_copy(j, i).start()

            return carry

        lax.fori_loop(0, PARTS, one, 0)

    def pair_copy(j, i):
        sl = pl.ds(pl.multiple_of(i * span, span), span)
        h = j // 2
        return remote(
            pair_out.at[h, sl], pair_in.at[h, sl], pair_send.at[h, i], pair_recv.at[h, i],
            at(g, mate, z),
        )

    def far_copy(i):
        sl = pl.ds(pl.multiple_of(i * span, span), span)
        return remote(
            far_out.at[sl], far_in.at[sl], far_send.at[i], far_recv.at[i],
            at(g, (1 - side) * 2 + core, z),
        )

    def pass_on(j):
        @pl.when((j % 2 == core) & (j // 2 != side))
        def _():
            def one(i, carry):
                sl = pl.ds(pl.multiple_of(i * span, span), span)
                pair_copy(j, i).wait_recv()
                total = acc[j, sl, :] + pair_in[j // 2, sl, :].astype(jnp.float32)
                far_out[sl, :] = total.astype(jnp.bfloat16)
                far_copy(i).start()
                return carry

            lax.fori_loop(0, PARTS, one, 0)

    def fan_copy(step):
        q = lax.rem(place + step, groups * rows)
        here = fitted.at[:, mine]
        return remote(
            here, here, fan_send.at[step - 1], fan_recv.at[step - 1], at(q // rows, q % rows, z)
        )

    for step in range(1, cols):
        fit_copy(step).wait_recv()
    for step in range(1, peers + 1):
        fan_copy(step).start()

    def ladder(k):
        left = own[k]
        total = jnp.zeros((virtual, virtual), jnp.float32)
        for p in range(cols):
            dressed = jnp.dot(fitted[p], left, preferred_element_type=jnp.float32)
            total += lax.dot_general(
                dressed.astype(jnp.bfloat16), fitted[p], NT, preferred_element_type=jnp.float32
            )
        own[k] = total.astype(jnp.bfloat16)

    own_hop = jnp.where(end_plane, 1, cols - 2)
    per_step = pairs // chunks

    def hop(n, carry):
        low, high = z - n, z + n

        def step(c, inner):
            on_time = jnp.logical_not(late_in & (n == 1) & (c >= half))
            has_low, has_high = (low >= 0) & on_time, (high < cols) & on_time

            @pl.when(has_low)
            def _():
                up_copy(low, c).wait_recv()

                @pl.when(z + 1 < cols)
                def _():
                    up_copy(low, c).start()

            @pl.when(has_high)
            def _():
                down_copy(high, c).wait_recv()

                @pl.when(z > 0)
                def _():
                    down_copy(high, c).start()

            @pl.when((n == cols - 2) & (c == chunks - 1))
            def _():
                @pl.when(late_up)
                def _():
                    for d in range(half, chunks):
                        up_copy(z, d).start()

                @pl.when(late_down)
                def _():
                    for d in range(half, chunks):
                        down_copy(z, d).start()

            @pl.when(n == 1)
            def _():
                load_weight(c).wait()

            @pl.when(has_low)
            def _():
                multiply(low, c)

            @pl.when(has_high)
            def _():
                multiply(high, c)

            @pl.when(n == own_hop)
            def _():
                multiply(z, c)

            @pl.when(n == own_hop + 1)
            def _():
                @pl.when(c == 0)
                def _():
                    for step in range(1, peers + 1):
                        fan_copy(step).wait_recv()

                for k in range(per_step):
                    ladder(c * per_step + k)

            return inner

        lax.fori_loop(0, chunks, step, 0)
        whole = jnp.logical_not(late_in & (n == 1))
        for j, valid in ((low, (low >= 0) & whole), (high, (high < cols) & whole), (z, n == own_hop)):
            @pl.when(valid)
            def _():
                pass_on(j)

        @pl.when(n == own_hop + 1)
        def _():
            pltpu.make_async_copy(own, ladder_out, load_sem.at[0]).start()

        return carry

    lax.fori_loop(1, cols, hop, 0)

    @pl.when(late_in)
    def _():
        def step(c, carry):
            piece = panel.at[late_block, c]
            remote(
                piece, piece, up_send.at[late_block, c], z_recv.at[late_block, c], at(g, mate, z)
            ).wait_recv()
            multiply(late_block, c)
            return carry

        lax.fori_loop(half, chunks, step, 0)

    def out_copy(i):
        return pltpu.make_async_copy(
            result.at[i], cycle_out.at[:, pl.ds(i * span, span)], out_sem.at[i]
        )

    for i in range(PARTS):
        sl = pl.ds(i * span, span)
        pair_copy(r, i).wait_recv()
        far_copy(i).wait_recv()
        total = acc[r, sl, :] + pair_in[side, sl, :].astype(jnp.float32)
        total += far_in[sl, :].astype(jnp.float32)
        result[i] = total.T.astype(jnp.bfloat16)
        out_copy(i).start()

    pltpu.make_async_copy(own, ladder_out, load_sem.at[0]).wait()
    for step in range(1, cols):
        fit_copy(step).wait_send()
    for step in range(1, peers + 1):
        fan_copy(step).wait_send()

    def drain(c, carry):
        for s in range(sides):
            raw_copy(c, s).wait_send()
            for q in range(groups):
                @pl.when(jnp.logical_not((q == g) & (s == side)))
                def _():
                    ex_copy(c, s, q).wait_send()
        for j in range(cols):
            @pl.when((j <= z) & (z + 1 < cols))
            def _():
                up_copy(j, c).wait_send()

            @pl.when((j >= z) & (z > 0))
            def _():
                down_copy(j, c).wait_send()
        return carry

    lax.fori_loop(0, chunks, drain, 0)
    for i in range(PARTS):
        for h in range(sides):
            pair_copy(2 * h, i).wait_send()
        far_copy(i).wait_send()
        out_copy(i).wait()


def hand_over(ladder_in, cycle_in, ladder_out, cycle_out, sem):
    moves = []
    for n, (source, target) in enumerate(((ladder_in, ladder_out), (cycle_in, cycle_out))):
        size = source.shape[0] // PARTS
        for i in range(PARTS):
            sl = pl.ds(i * size, size)
            moves.append(pltpu.make_async_copy(source.at[sl], target.at[sl], sem.at[n, i]))
    for move in moves:
        move.start()
    for move in moves:
        move.wait()


def fused_shards(sizes, amplitudes, factors, cycle_weight, orbital_order):
    groups, rows, cols = sizes
    pairs, one, virtual, _ = amplitudes.shape
    out_width, depth = cycle_weight.shape
    block = virtual // rows
    chunks = block // TILE
    chips = groups * rows // 2
    panel_width = virtual // groups
    span = out_width // PARTS
    half = jnp.bfloat16
    dma = pltpu.SemaphoreType.DMA
    anywhere = pl.BlockSpec(memory_space=pl.ANY)
    matmuls = 2 * out_width * depth * cols * panel_width
    ladder_term, cycle_term = pl.pallas_call(
        functools.partial(kernel, sizes),
        out_shape=(
            jax.ShapeDtypeStruct((pairs, virtual, virtual), half),
            jax.ShapeDtypeStruct((panel_width, out_width), half),
        ),
        in_specs=[pl.BlockSpec(memory_space=pltpu.VMEM), anywhere, anywhere, anywhere],
        out_specs=(anywhere, anywhere),
        scratch_shapes=[
            pltpu.VMEM((chunks, out_width, depth // chunks), half),
            pltpu.VMEM((pairs, virtual, virtual), half),
            pltpu.VMEM((chunks, rows // 2, pairs, TILE, virtual), half),
            pltpu.VMEM((chunks, rows // 2, groups, TILE, 2 * pairs, panel_width), half),
            pltpu.VMEM((cols, chunks, TILE, 2 * pairs * chips, panel_width), half),
            pltpu.VMEM((cols, out_width, panel_width), jnp.float32),
            pltpu.VMEM((rows // 2, out_width, panel_width), half),
            pltpu.VMEM((rows // 2, out_width, panel_width), half),
            pltpu.VMEM((out_width, panel_width), half),
            pltpu.VMEM((out_width, panel_width), half),
            pltpu.VMEM((PARTS, panel_width, span), half),
            pltpu.VMEM((cols, virtual, virtual), half),
            dma((2,)),
            dma((chunks,)),
            dma((chunks, rows // 2)),
            dma((chunks, rows // 2)),
            dma((chunks, chips)),
            dma((chunks, chips)),
            dma((cols, chunks)),
            dma((cols, chunks)),
            dma((cols, chunks)),
            dma((cols - 1,)),
            dma((cols - 1,)),
            dma((groups * rows - 1,)),
            dma((groups * rows - 1,)),
            dma((rows // 2, PARTS)),
            dma((rows // 2, PARTS)),
            dma((PARTS,)),
            dma((PARTS,)),
            dma((PARTS,)),
        ],
        compiler_params=pltpu.CompilerParams(
            collective_id=0, has_side_effects=True, vmem_limit_bytes=60 * 1024 * 1024
        ),
        cost_estimate=pl.CostEstimate(
            flops=matmuls, bytes_accessed=2 * out_width * depth, transcendentals=0
        ),
    )(
        orbital_order.reshape(1, virtual),
        amplitudes.reshape(pairs, virtual, virtual),
        factors,
        cycle_weight,
    )
    ladder_term, cycle_term = pl.pallas_call(
        hand_over,
        out_shape=(
            jax.ShapeDtypeStruct(ladder_term.shape, half),
            jax.ShapeDtypeStruct(cycle_term.shape, half),
        ),
        in_specs=[anywhere, anywhere],
        out_specs=(anywhere, anywhere),
        scratch_shapes=[dma((2, PARTS))],
        compiler_params=pltpu.CompilerParams(vmem_limit_bytes=60 * 1024 * 1024),
    )(ladder_term, cycle_term)
    return ladder_term.reshape(pairs, one, virtual, virtual), cycle_term


def shards(amplitudes, factors, cycle_weight, orbital_order):
    groups, rows, cols = (lax.axis_size(name) for name in ("grp", "row", "col"))
    pairs, per_col, virtual, _ = amplitudes.shape
    out_width, depth = cycle_weight.shape
    fits = (
        per_col == 1
        and factors.shape[0] == 1
        and rows == cols
        and rows // 2 == 2
        and rows % 2 == 0
        and 2 * pairs == TILE
        and virtual == groups * LANES
        and virtual % (rows * TILE) == 0
        and pairs % (virtual // (rows * TILE)) == 0
        and virtual // (rows * TILE) > 1
        and virtual % (groups * rows * TILE) == 0
        and depth == virtual // rows * groups * rows * pairs
        and out_width % (PARTS * LANES) == 0
        and 2 * out_width * depth <= 36 * 1024 * 1024
    )
    if fits:
        return fused_shards((groups, rows, cols), amplitudes, factors, cycle_weight, orbital_order)
    return plain_shards(amplitudes, factors, cycle_weight, orbital_order)


def solution(mesh):
    return jax.shard_map(
        shards,
        mesh=mesh,
        in_specs=(P(("grp", "row"), "col", None, None), P("col", None, None), P("col", "row"), P()),
        out_specs=(P(("grp", "row"), "col", None, None), P(("grp", "row"), "col")),
        check_vma=False,
    )
```

```python
import functools

import jax
import jax.numpy as jnp
from jax import lax
from jax.experimental import pallas as pl
from jax.experimental.pallas import tpu as pltpu
from jax.sharding import PartitionSpec as P

MESH = pl.DeviceIdType.MESH
TILE = 16
LANES = 128
PARTS = 4
NT = (((1,), (1,)), ((), ()))


def dress_pairs(factor_piece, pair_stack):
    dressed = jnp.einsum(
        "pac,qcd->pqad", factor_piece, pair_stack, preferred_element_type=jnp.float32
    ).astype(jnp.bfloat16)
    return jnp.einsum("pqad,pbd->qab", dressed, factor_piece, preferred_element_type=jnp.float32)


def plain_shards(amplitudes, factors, cycle_weight, orbital_order):
    occ_rows = amplitudes.shape[0]
    occ_cols = amplitudes.shape[1]
    virtual = amplitudes.shape[2]
    pair_stack = amplitudes.reshape(occ_rows * occ_cols, virtual, virtual)
    ladder_sum = dress_pairs(lax.all_gather(factors, "col", axis=0, tiled=True), pair_stack)
    ladder_sum = ladder_sum.reshape(occ_rows, occ_cols, virtual, virtual)
    ladder_term = ladder_sum.astype(jnp.bfloat16)
    groups = lax.axis_size("grp")
    row_count = lax.axis_size("row")
    panel_width = virtual // groups
    block_width = virtual // row_count
    ordered = jnp.take(amplitudes, orbital_order, axis=3)
    ordered = ordered.reshape(occ_rows, occ_cols, row_count, block_width, groups, panel_width)
    outgoing = jnp.transpose(ordered, (4, 2, 3, 0, 1, 5))
    outgoing = outgoing.reshape(groups * row_count, block_width, 1, occ_rows, occ_cols, panel_width)
    arrived = lax.all_to_all(outgoing, ("grp", "row"), split_axis=0, concat_axis=2, tiled=True)
    column_tile = arrived.reshape(
        block_width * groups * row_count * occ_rows, occ_cols * panel_width
    )
    products = lax.dot_general(
        lax.all_gather(column_tile, "col", axis=1, tiled=True),
        cycle_weight,
        (((0,), (1,)), ((), ())),
        preferred_element_type=jnp.float32,
    )
    cycle_term = lax.psum_scatter(products, "row", scatter_dimension=0, tiled=True).astype(
        jnp.bfloat16
    )
    return (ladder_term, cycle_term)


def kernel(
    sizes, order_ref, amp, fac, weight, ladder_out, cycle_out,
    wv, own, other, staged, panel, acc, pair_out, pair_in, far_out, far_in, result, fitted,
    load_sem, weight_sem, raw_send, raw_recv, ex_send, ex_recv, up_send, down_send, z_recv,
    fit_send, fit_recv, fan_send, fan_recv, pair_send, pair_recv, far_send, far_recv, out_sem,
):
    groups, rows, cols = sizes
    sides = rows // 2
    chips = groups * sides
    pairs, virtual, _ = amp.shape
    block = virtual // rows
    chunks = block // TILE
    depth = weight.shape[1] // chunks
    span = weight.shape[0] // PARTS
    panel_width = virtual // groups
    g, r, z = lax.axis_index("grp"), lax.axis_index("row"), lax.axis_index("col")
    side, core = r // 2, r % 2
    mate = side * 2 + 1 - core
    chip = g * sides + side
    place = g * rows + r
    fit_rows = virtual // (groups * rows)

    def at(gg, rr, zz):
        return {"grp": gg, "row": rr, "col": zz}

    def remote(src, dst, send, recv, where):
        return pltpu.make_async_remote_copy(
            src_ref=src, dst_ref=dst, send_sem=send, recv_sem=recv,
            device_id=where, device_id_type=MESH,
        )

    mine = pl.ds(pl.multiple_of(place * fit_rows, fit_rows), fit_rows)
    load_own = pltpu.make_async_copy(amp, own, load_sem.at[0])
    load_own.start()
    load_fit = pltpu.make_async_copy(fac.at[0, mine], fitted.at[z, mine], load_sem.at[1])
    load_fit.start()

    def load_weight(c):
        return pltpu.make_async_copy(
            weight.at[:, pl.ds(c * depth, depth)], wv.at[c], weight_sem.at[c]
        )

    for c in range(chunks):
        load_weight(c).start()

    peers = groups * rows - 1
    barrier = pltpu.get_barrier_semaphore()
    for step in range(1, peers + 1):
        q = lax.rem(place + step, groups * rows)
        pl.semaphore_signal(barrier, inc=1, device_id=at(q // rows, q % rows, z), device_id_type=MESH)
    for step in range(1, cols):
        pl.semaphore_signal(
            barrier, inc=1, device_id=at(g, r, lax.rem(z + step, cols)), device_id_type=MESH
        )
    pl.semaphore_wait(barrier, peers + cols - 1)

    def raw_copy(c, s):
        first = pl.multiple_of((s * 2 + 1 - core) * block + c * TILE, TILE)
        return remote(
            amp.at[:, pl.ds(first, TILE)], other.at[c, s], raw_send.at[c, s], raw_recv.at[c, s],
            at(g, mate, z),
        )

    for c in range(chunks):
        for s in range(sides):
            raw_copy(c, s).start()

    load_fit.wait()

    def fit_copy(step):
        here = fitted.at[z, mine]
        return remote(
            here, here, fit_send.at[step - 1], fit_recv.at[step - 1],
            at(g, r, lax.rem(z + step, cols)),
        )

    for step in range(1, cols):
        fit_copy(step).start()

    load_own.wait()

    width = 2 * pairs * TILE
    pick = (
        lax.broadcasted_iota(jnp.int32, (virtual, virtual), 0) == order_ref[...]
    ).astype(jnp.float32).astype(jnp.bfloat16)
    to_row = lax.broadcasted_iota(jnp.int32, (width, width), 0)
    from_row = lax.broadcasted_iota(jnp.int32, (width, width), 1)
    k_row = to_row & (2 * pairs - 1)
    c_row = to_row // (2 * pairs)
    late = (k_row // pairs) ^ core
    turn = (
        from_row == late * (pairs * TILE) + (k_row & (pairs - 1)) * TILE + c_row
    ).astype(jnp.float32).astype(jnp.bfloat16)

    slot = pl.ds(pl.multiple_of(chip * TILE, TILE), TILE)

    def ex_copy(c, s, q):
        return remote(
            staged.at[c, s, q], panel.at[z, c, :, slot, :],
            ex_send.at[c, s * groups + q], ex_recv.at[c, chip], at(q, s * 2 + core, z),
        )

    end_plane = (z == 0) | (z == cols - 1)
    late_block = jnp.where(z == 0, 1, cols - 2)
    late_in = end_plane & (late_block // 2 == side)
    late_up = (z == cols - 2) & ((cols - 2) // 2 == side)
    late_down = (z == 1) & (1 // 2 == side)
    half = chunks // 2

    def up_copy(j, c):
        piece = panel.at[j, c]
        return remote(piece, piece, up_send.at[j, c], z_recv.at[j, c], at(g, r, z + 1))

    def down_copy(j, c):
        piece = panel.at[j, c]
        return remote(piece, piece, down_send.at[j, c], z_recv.at[j, c], at(g, r, z - 1))

    def send_own(c):
        for q in range(chips):
            @pl.when(q != chip)
            def _():
                landing = panel.at[z, c, :, pl.ds(q * TILE, TILE), :]
                remote(
                    landing, landing, ex_send.at[c, 0], ex_recv.at[c, q], at(g, mate, z)
                ).wait_recv()

        @pl.when((z + 1 < cols) & jnp.logical_not(late_up & (c >= half)))
        def _():
            up_copy(z, c).start()

        @pl.when((z > 0) & jnp.logical_not(late_down & (c >= half)))
        def _():
            down_copy(z, c).start()

    def exchange(c, carry):
        for s in range(sides):
            raw_copy(c, s).wait_recv()
        for s in range(sides):
            first = pl.multiple_of((s * 2 + core) * block + c * TILE, TILE)
            near = own[:, pl.ds(first, TILE), :].reshape(pairs * TILE, virtual)
            far = other[c, s].reshape(pairs * TILE, virtual)
            both = jnp.concatenate([near, far], axis=0)
            picked = jnp.dot(both, pick, preferred_element_type=jnp.float32).astype(jnp.bfloat16)
            turned = jnp.dot(turn, picked, preferred_element_type=jnp.float32).astype(jnp.bfloat16)
            for q in range(groups):
                part = turned[:, q * panel_width:(q + 1) * panel_width]
                part = part.reshape(TILE, 2 * pairs, panel_width)
                here = (q == g) & (s == side)

                @pl.when(here)
                def _():
                    panel[z, c, :, slot, :] = part

                @pl.when(jnp.logical_not(here))
                def _():
                    staged[c, s, q] = part
                    ex_copy(c, s, q).start()

        @pl.when(c > 0)
        def _():
            send_own(c - 1)

        return carry

    lax.fori_loop(0, chunks, exchange, 0)
    send_own(chunks - 1)

    def multiply(blocks, c):
        piece = jnp.concatenate([panel[j, c].reshape(depth, panel_width) for j in blocks], axis=1)

        def one(i, carry):
            sl = pl.ds(pl.multiple_of(i * span, span), span)
            product = jnp.dot(wv[c, sl, :], piece, preferred_element_type=jnp.float32)
            for n, j in enumerate(blocks):
                part = product[:, n * panel_width:(n + 1) * panel_width]

                @pl.when(c == 0)
                def _():
                    acc[j, sl, :] = part

                @pl.when(c > 0)
                def _():
                    acc[j, sl, :] += part

                @pl.when((c == chunks - 1) & (j % 2 != core))
                def _():
                    pair_out[j // 2, sl, :] = acc[j, sl, :].astype(jnp.bfloat16)
                    pair_copy(j, i).start()

            return carry

        lax.fori_loop(0, PARTS, one, 0)

    def pair_copy(j, i):
        sl = pl.ds(pl.multiple_of(i * span, span), span)
        h = j // 2
        return remote(
            pair_out.at[h, sl], pair_in.at[h, sl], pair_send.at[h, i], pair_recv.at[h, i],
            at(g, mate, z),
        )

    def far_copy(i):
        sl = pl.ds(pl.multiple_of(i * span, span), span)
        return remote(
            far_out.at[sl], far_in.at[sl], far_send.at[i], far_recv.at[i],
            at(g, (1 - side) * 2 + core, z),
        )

    def pass_on(j):
        @pl.when((j % 2 == core) & (j // 2 != side))
        def _():
            def one(i, carry):
                sl = pl.ds(pl.multiple_of(i * span, span), span)
                pair_copy(j, i).wait_recv()
                total = acc[j, sl, :] + pair_in[j // 2, sl, :].astype(jnp.float32)
                far_out[sl, :] = total.astype(jnp.bfloat16)
                far_copy(i).start()
                return carry

            lax.fori_loop(0, PARTS, one, 0)

    def fan_copy(step):
        q = lax.rem(place + step, groups * rows)
        here = fitted.at[:, mine]
        return remote(
            here, here, fan_send.at[step - 1], fan_recv.at[step - 1], at(q // rows, q % rows, z)
        )

    for step in range(1, cols):
        fit_copy(step).wait_recv()
    for step in range(1, peers + 1):
        fan_copy(step).start()

    def ladder(k):
        left = own[k]
        total = jnp.zeros((virtual, virtual), jnp.float32)
        for p in range(cols):
            dressed = jnp.dot(fitted[p], left, preferred_element_type=jnp.float32)
            total += lax.dot_general(
                dressed.astype(jnp.bfloat16), fitted[p], NT, preferred_element_type=jnp.float32
            )
        own[k] = total.astype(jnp.bfloat16)

    own_hop = jnp.where(end_plane, 1, cols - 2)
    per_step = pairs // chunks

    def hop(n, carry):
        low, high = z - n, z + n

        def step(c, inner):
            on_time = jnp.logical_not(late_in & (n == 1) & (c >= half))
            has_low, has_high = (low >= 0) & on_time, (high < cols) & on_time

            @pl.when(has_low)
            def _():
                up_copy(low, c).wait_recv()

                @pl.when(z + 1 < cols)
                def _():
                    up_copy(low, c).start()

            @pl.when(has_high)
            def _():
                down_copy(high, c).wait_recv()

                @pl.when(z > 0)
                def _():
                    down_copy(high, c).start()

            @pl.when((n == cols - 2) & (c == chunks - 1))
            def _():
                @pl.when(late_up)
                def _():
                    for d in range(half, chunks):
                        up_copy(z, d).start()

                @pl.when(late_down)
                def _():
                    for d in range(half, chunks):
                        down_copy(z, d).start()

            @pl.when(n == 1)
            def _():
                load_weight(c).wait()

            inside = (n == 1) & jnp.logical_not(end_plane)
            other = jnp.where(low >= 0, low, high)

            @pl.when(inside | ((n == own_hop) & on_time))
            def _():
                multiply((jnp.where(inside, low, z), jnp.where(inside, high, other)), c)

            @pl.when(end_plane & ((n > 1) | jnp.logical_not(on_time)))
            def _():
                multiply((jnp.where(n > 1, other, z),), c)

            @pl.when(n == own_hop + 1)
            def _():
                @pl.when(c == 0)
                def _():
                    for step in range(1, peers + 1):
                        fan_copy(step).wait_recv()

                for k in range(per_step):
                    ladder(c * per_step + k)

            return inner

        lax.fori_loop(0, chunks, step, 0)
        whole = jnp.logical_not(late_in & (n == 1))
        for j, valid in ((low, (low >= 0) & whole), (high, (high < cols) & whole), (z, n == own_hop)):
            @pl.when(valid)
            def _():
                pass_on(j)

        @pl.when(n == own_hop + 1)
        def _():
            pltpu.make_async_copy(own, ladder_out, load_sem.at[0]).start()

        return carry

    lax.fori_loop(1, cols, hop, 0)

    @pl.when(late_in)
    def _():
        def step(c, carry):
            piece = panel.at[late_block, c]
            remote(
                piece, piece, up_send.at[late_block, c], z_recv.at[late_block, c], at(g, mate, z)
            ).wait_recv()
            multiply((late_block,), c)
            return carry

        lax.fori_loop(half, chunks, step, 0)

    def out_copy(i):
        return pltpu.make_async_copy(
            result.at[i], cycle_out.at[:, pl.ds(i * span, span)], out_sem.at[i]
        )

    for i in range(PARTS):
        sl = pl.ds(i * span, span)
        pair_copy(r, i).wait_recv()
        far_copy(i).wait_recv()
        total = acc[r, sl, :] + pair_in[side, sl, :].astype(jnp.float32)
        total += far_in[sl, :].astype(jnp.float32)
        result[i] = total.astype(jnp.bfloat16).T
        out_copy(i).start()

    pltpu.make_async_copy(own, ladder_out, load_sem.at[0]).wait()
    for step in range(1, cols):
        fit_copy(step).wait_send()
    for step in range(1, peers + 1):
        fan_copy(step).wait_send()

    def drain(c, carry):
        for s in range(sides):
            raw_copy(c, s).wait_send()
            for q in range(groups):
                @pl.when(jnp.logical_not((q == g) & (s == side)))
                def _():
                    ex_copy(c, s, q).wait_send()
        for j in range(cols):
            @pl.when((j <= z) & (z + 1 < cols))
            def _():
                up_copy(j, c).wait_send()

            @pl.when((j >= z) & (z > 0))
            def _():
                down_copy(j, c).wait_send()
        return carry

    lax.fori_loop(0, chunks, drain, 0)
    for i in range(PARTS):
        for h in range(sides):
            pair_copy(2 * h, i).wait_send()
        far_copy(i).wait_send()
        out_copy(i).wait()


def hand_over(ladder_in, cycle_in, ladder_out, cycle_out, ladder_held, cycle_held, sem):
    fetches, stores = [], []
    whole = ((ladder_in, ladder_held, ladder_out), (cycle_in, cycle_held, cycle_out))
    for n, (source, held, target) in enumerate(whole):
        size = source.shape[0] // PARTS
        for i in range(PARTS):
            sl = pl.ds(i * size, size)
            fetches.append(pltpu.make_async_copy(source.at[sl], held.at[sl], sem.at[0, n, i]))
            stores.append(pltpu.make_async_copy(held.at[sl], target.at[sl], sem.at[1, n, i]))
    for fetch in fetches:
        fetch.start()
    for fetch, store in zip(fetches, stores):
        fetch.wait()
        store.start()
    for store in stores:
        store.wait()


def fused_shards(sizes, amplitudes, factors, cycle_weight, orbital_order):
    groups, rows, cols = sizes
    pairs, one, virtual, _ = amplitudes.shape
    out_width, depth = cycle_weight.shape
    block = virtual // rows
    chunks = block // TILE
    chips = groups * rows // 2
    panel_width = virtual // groups
    span = out_width // PARTS
    half = jnp.bfloat16
    dma = pltpu.SemaphoreType.DMA
    anywhere = pl.BlockSpec(memory_space=pl.ANY)
    matmuls = 2 * out_width * depth * cols * panel_width
    ladder_term, cycle_term = pl.pallas_call(
        functools.partial(kernel, sizes),
        out_shape=(
            jax.ShapeDtypeStruct((pairs, virtual, virtual), half),
            jax.ShapeDtypeStruct((panel_width, out_width), half),
        ),
        in_specs=[pl.BlockSpec(memory_space=pltpu.VMEM), anywhere, anywhere, anywhere],
        out_specs=(anywhere, anywhere),
        scratch_shapes=[
            pltpu.VMEM((chunks, out_width, depth // chunks), half),
            pltpu.VMEM((pairs, virtual, virtual), half),
            pltpu.VMEM((chunks, rows // 2, pairs, TILE, virtual), half),
            pltpu.VMEM((chunks, rows // 2, groups, TILE, 2 * pairs, panel_width), half),
            pltpu.VMEM((cols, chunks, TILE, 2 * pairs * chips, panel_width), half),
            pltpu.VMEM((cols, out_width, panel_width), jnp.float32),
            pltpu.VMEM((rows // 2, out_width, panel_width), half),
            pltpu.VMEM((rows // 2, out_width, panel_width), half),
            pltpu.VMEM((out_width, panel_width), half),
            pltpu.VMEM((out_width, panel_width), half),
            pltpu.VMEM((PARTS, panel_width, span), half),
            pltpu.VMEM((cols, virtual, virtual), half),
            dma((2,)),
            dma((chunks,)),
            dma((chunks, rows // 2)),
            dma((chunks, rows // 2)),
            dma((chunks, chips)),
            dma((chunks, chips)),
            dma((cols, chunks)),
            dma((cols, chunks)),
            dma((cols, chunks)),
            dma((cols - 1,)),
            dma((cols - 1,)),
            dma((groups * rows - 1,)),
            dma((groups * rows - 1,)),
            dma((rows // 2, PARTS)),
            dma((rows // 2, PARTS)),
            dma((PARTS,)),
            dma((PARTS,)),
            dma((PARTS,)),
        ],
        compiler_params=pltpu.CompilerParams(
            collective_id=0, has_side_effects=True, vmem_limit_bytes=60 * 1024 * 1024
        ),
        cost_estimate=pl.CostEstimate(
            flops=matmuls, bytes_accessed=2 * out_width * depth, transcendentals=0
        ),
    )(
        orbital_order.reshape(1, virtual),
        amplitudes.reshape(pairs, virtual, virtual),
        factors,
        cycle_weight,
    )
    ladder_term, cycle_term = pl.pallas_call(
        hand_over,
        out_shape=(
            jax.ShapeDtypeStruct(ladder_term.shape, half),
            jax.ShapeDtypeStruct(cycle_term.shape, half),
        ),
        in_specs=[anywhere, anywhere],
        out_specs=(anywhere, anywhere),
        scratch_shapes=[
            pltpu.VMEM(ladder_term.shape, half),
            pltpu.VMEM(cycle_term.shape, half),
            dma((2, 2, PARTS)),
        ],
        compiler_params=pltpu.CompilerParams(vmem_limit_bytes=60 * 1024 * 1024),
    )(ladder_term, cycle_term)
    return ladder_term.reshape(pairs, one, virtual, virtual), cycle_term


def shards(amplitudes, factors, cycle_weight, orbital_order):
    groups, rows, cols = (lax.axis_size(name) for name in ("grp", "row", "col"))
    pairs, per_col, virtual, _ = amplitudes.shape
    out_width, depth = cycle_weight.shape
    fits = (
        per_col == 1
        and factors.shape[0] == 1
        and rows == cols
        and rows // 2 == 2
        and rows % 2 == 0
        and 2 * pairs == TILE
        and virtual == groups * LANES
        and virtual % (rows * TILE) == 0
        and pairs % (virtual // (rows * TILE)) == 0
        and virtual // (rows * TILE) > 1
        and virtual % (groups * rows * TILE) == 0
        and depth == virtual // rows * groups * rows * pairs
        and out_width % (PARTS * LANES) == 0
        and 2 * out_width * depth <= 36 * 1024 * 1024
    )
    if fits:
        return fused_shards((groups, rows, cols), amplitudes, factors, cycle_weight, orbital_order)
    return plain_shards(amplitudes, factors, cycle_weight, orbital_order)


def solution(mesh):
    return jax.shard_map(
        shards,
        mesh=mesh,
        in_specs=(P(("grp", "row"), "col", None, None), P("col", None, None), P("col", "row"), P()),
        out_specs=(P(("grp", "row"), "col", None, None), P(("grp", "row"), "col")),
        check_vma=False,
    )
```

```python
import functools

import jax
import jax.numpy as jnp
from jax import lax
from jax.experimental import pallas as pl
from jax.experimental.pallas import tpu as pltpu
from jax.sharding import PartitionSpec as P

MESH = pl.DeviceIdType.MESH
TILE = 16
LANES = 128
PARTS = 4
NT = (((1,), (1,)), ((), ()))


def dress_pairs(factor_piece, pair_stack):
    dressed = jnp.einsum(
        "pac,qcd->pqad", factor_piece, pair_stack, preferred_element_type=jnp.float32
    ).astype(jnp.bfloat16)
    return jnp.einsum("pqad,pbd->qab", dressed, factor_piece, preferred_element_type=jnp.float32)


def plain_shards(amplitudes, factors, cycle_weight, orbital_order):
    occ_rows = amplitudes.shape[0]
    occ_cols = amplitudes.shape[1]
    virtual = amplitudes.shape[2]
    pair_stack = amplitudes.reshape(occ_rows * occ_cols, virtual, virtual)
    ladder_sum = dress_pairs(lax.all_gather(factors, "col", axis=0, tiled=True), pair_stack)
    ladder_sum = ladder_sum.reshape(occ_rows, occ_cols, virtual, virtual)
    ladder_term = ladder_sum.astype(jnp.bfloat16)
    groups = lax.axis_size("grp")
    row_count = lax.axis_size("row")
    panel_width = virtual // groups
    block_width = virtual // row_count
    ordered = jnp.take(amplitudes, orbital_order, axis=3)
    ordered = ordered.reshape(occ_rows, occ_cols, row_count, block_width, groups, panel_width)
    outgoing = jnp.transpose(ordered, (4, 2, 3, 0, 1, 5))
    outgoing = outgoing.reshape(groups * row_count, block_width, 1, occ_rows, occ_cols, panel_width)
    arrived = lax.all_to_all(outgoing, ("grp", "row"), split_axis=0, concat_axis=2, tiled=True)
    column_tile = arrived.reshape(
        block_width * groups * row_count * occ_rows, occ_cols * panel_width
    )
    products = lax.dot_general(
        lax.all_gather(column_tile, "col", axis=1, tiled=True),
        cycle_weight,
        (((0,), (1,)), ((), ())),
        preferred_element_type=jnp.float32,
    )
    cycle_term = lax.psum_scatter(products, "row", scatter_dimension=0, tiled=True).astype(
        jnp.bfloat16
    )
    return (ladder_term, cycle_term)


def kernel(
    sizes, order_ref, amp, fac, weight, ladder_out, cycle_out,
    wv, own, other, staged, panel, acc, pair_out, pair_in, far_out, far_in, result, fitted,
    load_sem, weight_sem, raw_send, raw_recv, ex_send, ex_recv, up_send, down_send, z_recv,
    fit_send, fit_recv, fan_send, fan_recv, pair_send, pair_recv, far_send, far_recv, out_sem,
):
    groups, rows, cols = sizes
    sides = rows // 2
    chips = groups * sides
    pairs, virtual, _ = amp.shape
    block = virtual // rows
    chunks = block // TILE
    depth = weight.shape[1] // chunks
    span = weight.shape[0] // PARTS
    panel_width = virtual // groups
    g, r, z = lax.axis_index("grp"), lax.axis_index("row"), lax.axis_index("col")
    side, core = r // 2, r % 2
    mate = side * 2 + 1 - core
    chip = g * sides + side
    place = g * rows + r
    fit_rows = virtual // (groups * rows)

    def at(gg, rr, zz):
        return {"grp": gg, "row": rr, "col": zz}

    def remote(src, dst, send, recv, where):
        return pltpu.make_async_remote_copy(
            src_ref=src, dst_ref=dst, send_sem=send, recv_sem=recv,
            device_id=where, device_id_type=MESH,
        )

    mine = pl.ds(pl.multiple_of(place * fit_rows, fit_rows), fit_rows)
    load_own = pltpu.make_async_copy(amp, own, load_sem.at[0])
    load_own.start()
    load_fit = pltpu.make_async_copy(fac.at[0, mine], fitted.at[z, mine], load_sem.at[1])
    load_fit.start()

    def load_weight(c):
        return pltpu.make_async_copy(
            weight.at[:, pl.ds(c * depth, depth)], wv.at[c], weight_sem.at[c]
        )

    for c in range(chunks):
        load_weight(c).start()

    peers = groups * rows - 1
    barrier = pltpu.get_barrier_semaphore()
    for step in range(1, peers + 1):
        q = lax.rem(place + step, groups * rows)
        pl.semaphore_signal(barrier, inc=1, device_id=at(q // rows, q % rows, z), device_id_type=MESH)
    for step in range(1, cols):
        pl.semaphore_signal(
            barrier, inc=1, device_id=at(g, r, lax.rem(z + step, cols)), device_id_type=MESH
        )
    pl.semaphore_wait(barrier, peers + cols - 1)

    def raw_copy(c, s):
        first = pl.multiple_of((s * 2 + 1 - core) * block + c * TILE, TILE)
        return remote(
            amp.at[:, pl.ds(first, TILE)], other.at[c, s], raw_send.at[c, s], raw_recv.at[c, s],
            at(g, mate, z),
        )

    for c in range(chunks):
        for s in range(sides):
            raw_copy(c, s).start()

    load_fit.wait()

    def fit_copy(step):
        here = fitted.at[z, mine]
        return remote(
            here, here, fit_send.at[step - 1], fit_recv.at[step - 1],
            at(g, r, lax.rem(z + step, cols)),
        )

    for step in range(1, cols):
        fit_copy(step).start()

    load_own.wait()

    width = 2 * pairs * TILE
    pick = (
        lax.broadcasted_iota(jnp.int32, (virtual, virtual), 0) == order_ref[...]
    ).astype(jnp.float32).astype(jnp.bfloat16)
    to_row = lax.broadcasted_iota(jnp.int32, (width, width), 0)
    from_row = lax.broadcasted_iota(jnp.int32, (width, width), 1)
    k_row = to_row & (2 * pairs - 1)
    c_row = to_row // (2 * pairs)
    late = (k_row // pairs) ^ core
    turn = (
        from_row == late * (pairs * TILE) + (k_row & (pairs - 1)) * TILE + c_row
    ).astype(jnp.float32).astype(jnp.bfloat16)

    slot = pl.ds(pl.multiple_of(chip * TILE, TILE), TILE)

    def ex_copy(c, s, q):
        return remote(
            staged.at[c, s, q], panel.at[z, c, :, slot, :],
            ex_send.at[c, s * groups + q], ex_recv.at[c, chip], at(q, s * 2 + core, z),
        )

    end_plane = (z == 0) | (z == cols - 1)
    late_block = jnp.where(z == 0, 1, cols - 2)
    late_in = end_plane & (late_block // 2 == side)
    late_up = (z == cols - 2) & ((cols - 2) // 2 == side)
    late_down = (z == 1) & (1 // 2 == side)
    half = chunks // 2

    fine = TILE // chips

    def piece_of(j, c, f, striped):
        if striped:
            return panel.at[j, c, :, pl.ds(pl.multiple_of(f * TILE, TILE), TILE), :]
        return panel.at[j, c, pl.ds(f * fine, fine)]

    def up_copy(j, c, f, striped):
        piece = piece_of(j, c, f, striped)
        return remote(piece, piece, up_send.at[j, c, f], z_recv.at[j, c, f], at(g, r, z + 1))

    def down_copy(j, c, f, striped):
        piece = piece_of(j, c, f, striped)
        return remote(piece, piece, down_send.at[j, c, f], z_recv.at[j, c, f], at(g, r, z - 1))

    def for_pieces(c, act):
        @pl.when(c == 0)
        def _():
            for i in range(chips):
                act(lax.rem(chip + i, chips), True)

        @pl.when(c > 0)
        def _():
            for f in range(chips):
                act(f, False)

    def arrived(c, q):
        @pl.when(q != chip)
        def _():
            landing = piece_of(z, c, q, True)
            remote(
                landing, landing, ex_send.at[c, 0], ex_recv.at[c, q], at(g, mate, z)
            ).wait_recv()

    def send_piece(c, f, striped):
        @pl.when((z + 1 < cols) & jnp.logical_not(late_up & (c >= half)))
        def _():
            up_copy(z, c, f, striped).start()

        @pl.when((z > 0) & jnp.logical_not(late_down & (c >= half)))
        def _():
            down_copy(z, c, f, striped).start()

    def send_own(c):
        @pl.when(c == 0)
        def _():
            for i in range(1, chips):
                q = lax.rem(chip + i, chips)
                arrived(0, q)
                send_piece(0, q, True)

        @pl.when(c > 0)
        def _():
            for q in range(chips):
                arrived(c, q)
            for f in range(chips):
                send_piece(c, f, False)

    def exchange(c, carry):
        for s in range(sides):
            raw_copy(c, s).wait_recv()
        for s in range(sides):
            first = pl.multiple_of((s * 2 + core) * block + c * TILE, TILE)
            near = own[:, pl.ds(first, TILE), :].reshape(pairs * TILE, virtual)
            far = other[c, s].reshape(pairs * TILE, virtual)
            both = jnp.concatenate([near, far], axis=0)
            picked = jnp.dot(both, pick, preferred_element_type=jnp.float32).astype(jnp.bfloat16)
            turned = jnp.dot(turn, picked, preferred_element_type=jnp.float32).astype(jnp.bfloat16)
            for q in range(groups):
                part = turned[:, q * panel_width:(q + 1) * panel_width]
                part = part.reshape(TILE, 2 * pairs, panel_width)
                here = (q == g) & (s == side)

                @pl.when(here)
                def _():
                    panel[z, c, :, slot, :] = part

                @pl.when(jnp.logical_not(here))
                def _():
                    staged[c, s, q] = part
                    ex_copy(c, s, q).start()

        @pl.when(c == 0)
        def _():
            send_piece(0, chip, True)

        @pl.when(c > 0)
        def _():
            send_own(c - 1)

        return carry

    lax.fori_loop(0, chunks, exchange, 0)
    send_own(jnp.int32(chunks - 1))

    def multiply(blocks, c, f=None):
        if f is None:
            wide, start, last = depth, 0, True
            held = [panel[j, c].reshape(depth, panel_width) for j in blocks]
        else:
            wide, last = depth // chips, f == chips - 1
            start = pl.multiple_of(f * wide, wide)
            held = [panel[j, c, pl.ds(f * fine, fine)].reshape(wide, panel_width) for j in blocks]
        piece = jnp.concatenate(held, axis=1)

        def one(i, carry):
            sl = pl.ds(pl.multiple_of(i * span, span), span)
            product = jnp.dot(
                wv[c, sl, pl.ds(start, wide)], piece, preferred_element_type=jnp.float32
            )
            for n, j in enumerate(blocks):
                part = product[:, n * panel_width:(n + 1) * panel_width]

                @pl.when(c == 0)
                def _():
                    acc[j, sl, :] = part

                @pl.when(c > 0)
                def _():
                    acc[j, sl, :] += part

                @pl.when((c == chunks - 1) & last & (j % 2 != core))
                def _():
                    pair_out[j // 2, sl, :] = acc[j, sl, :].astype(jnp.bfloat16)
                    pair_copy(j, i).start()

            return carry

        lax.fori_loop(0, PARTS, one, 0)

    def pair_copy(j, i):
        sl = pl.ds(pl.multiple_of(i * span, span), span)
        h = j // 2
        return remote(
            pair_out.at[h, sl], pair_in.at[h, sl], pair_send.at[h, i], pair_recv.at[h, i],
            at(g, mate, z),
        )

    def far_copy(i):
        sl = pl.ds(pl.multiple_of(i * span, span), span)
        return remote(
            far_out.at[sl], far_in.at[sl], far_send.at[i], far_recv.at[i],
            at(g, (1 - side) * 2 + core, z),
        )

    def pass_on(j):
        @pl.when((j % 2 == core) & (j // 2 != side))
        def _():
            def one(i, carry):
                sl = pl.ds(pl.multiple_of(i * span, span), span)
                pair_copy(j, i).wait_recv()
                total = acc[j, sl, :] + pair_in[j // 2, sl, :].astype(jnp.float32)
                far_out[sl, :] = total.astype(jnp.bfloat16)
                far_copy(i).start()
                return carry

            lax.fori_loop(0, PARTS, one, 0)

    def fan_copy(step):
        q = lax.rem(place + step, groups * rows)
        here = fitted.at[:, mine]
        return remote(
            here, here, fan_send.at[step - 1], fan_recv.at[step - 1], at(q // rows, q % rows, z)
        )

    for step in range(1, cols):
        fit_copy(step).wait_recv()
    for step in range(1, peers + 1):
        fan_copy(step).start()

    def ladder(k):
        left = own[k]
        total = jnp.zeros((virtual, virtual), jnp.float32)
        for p in range(cols):
            dressed = jnp.dot(fitted[p], left, preferred_element_type=jnp.float32)
            total += lax.dot_general(
                dressed.astype(jnp.bfloat16), fitted[p], NT, preferred_element_type=jnp.float32
            )
        own[k] = total.astype(jnp.bfloat16)

    own_hop = jnp.where(end_plane, 1, cols - 2)
    per_step = pairs // chunks

    def await_piece(j, c, f):
        piece = piece_of(j, c, f, False)
        remote(piece, piece, up_send.at[j, c, f], z_recv.at[j, c, f], at(g, mate, z)).wait_recv()

    def finish(j):
        c = jnp.int32(chunks - 1)

        def one(f, carry):
            await_piece(j, c, f)
            multiply((j,), c, f)
            return carry

        lax.fori_loop(0, chips, one, 0)

    def hop(n, carry):
        low, high = z - n, z + n

        def step(c, inner):
            on_time = jnp.logical_not(late_in & (n == 1) & (c >= half))
            has_low, has_high = (low >= 0) & on_time, (high < cols) & on_time

            ending = end_plane & (n == cols - 1) & (c == chunks - 1) & jnp.logical_not(late_in)

            @pl.when(has_low & jnp.logical_not(ending))
            def _():
                def act(f, striped):
                    up_copy(low, c, f, striped).wait_recv()

                    @pl.when(z + 1 < cols)
                    def _():
                        up_copy(low, c, f, striped).start()

                for_pieces(c, act)

            @pl.when(has_high & jnp.logical_not(ending))
            def _():
                def act(f, striped):
                    down_copy(high, c, f, striped).wait_recv()

                    @pl.when(z > 0)
                    def _():
                        down_copy(high, c, f, striped).start()

                for_pieces(c, act)

            @pl.when((n == cols - 2) & (c == chunks - 1))
            def _():
                for late, copy in ((late_up, up_copy), (late_down, down_copy)):
                    @pl.when(late)
                    def _():
                        for d in range(half, chunks):
                            for f in range(chips):
                                copy(z, d, f, False).start()

            @pl.when(n == 1)
            def _():
                load_weight(c).wait()

            inside = (n == 1) & jnp.logical_not(end_plane)
            other = jnp.where(low >= 0, low, high)

            @pl.when(inside | ((n == own_hop) & on_time))
            def _():
                multiply((jnp.where(inside, low, z), jnp.where(inside, high, other)), c)

            @pl.when(end_plane & ((n > 1) | jnp.logical_not(on_time)) & jnp.logical_not(ending))
            def _():
                multiply((jnp.where(n > 1, other, z),), c)

            @pl.when(ending)
            def _():
                finish(other)

            @pl.when(n == own_hop + 1)
            def _():
                @pl.when(c == 0)
                def _():
                    for step in range(1, peers + 1):
                        fan_copy(step).wait_recv()

                for k in range(per_step):
                    ladder(c * per_step + k)

            return inner

        lax.fori_loop(0, chunks, step, 0)
        whole = jnp.logical_not(late_in & (n == 1))
        for j, valid in ((low, (low >= 0) & whole), (high, (high < cols) & whole), (z, n == own_hop)):
            @pl.when(valid)
            def _():
                pass_on(j)

        @pl.when(n == own_hop + 1)
        def _():
            pltpu.make_async_copy(own, ladder_out, load_sem.at[0]).start()

        return carry

    lax.fori_loop(1, cols, hop, 0)

    @pl.when(late_in)
    def _():
        def step(c, carry):
            for f in range(chips):
                await_piece(late_block, c, f)
            multiply((late_block,), c)
            return carry

        lax.fori_loop(half, chunks - 1, step, 0)
        finish(late_block)

    def out_copy(i):
        return pltpu.make_async_copy(
            result.at[i], cycle_out.at[:, pl.ds(i * span, span)], out_sem.at[i]
        )

    for i in range(PARTS):
        sl = pl.ds(i * span, span)
        pair_copy(r, i).wait_recv()
        far_copy(i).wait_recv()
        total = acc[r, sl, :] + pair_in[side, sl, :].astype(jnp.float32)
        total += far_in[sl, :].astype(jnp.float32)
        result[i] = total.astype(jnp.bfloat16).T
        out_copy(i).start()

    pltpu.make_async_copy(own, ladder_out, load_sem.at[0]).wait()
    for step in range(1, cols):
        fit_copy(step).wait_send()
    for step in range(1, peers + 1):
        fan_copy(step).wait_send()

    def drain(c, carry):
        for s in range(sides):
            raw_copy(c, s).wait_send()
            for q in range(groups):
                @pl.when(jnp.logical_not((q == g) & (s == side)))
                def _():
                    ex_copy(c, s, q).wait_send()
        for j in range(cols):
            @pl.when((j <= z) & (z + 1 < cols))
            def _():
                for_pieces(c, lambda f, striped: up_copy(j, c, f, striped).wait_send())

            @pl.when((j >= z) & (z > 0))
            def _():
                for_pieces(c, lambda f, striped: down_copy(j, c, f, striped).wait_send())
        return carry

    lax.fori_loop(0, chunks, drain, 0)
    for i in range(PARTS):
        for h in range(sides):
            pair_copy(2 * h, i).wait_send()
        far_copy(i).wait_send()
        out_copy(i).wait()


def hand_over(ladder_in, cycle_in, ladder_out, cycle_out, ladder_held, cycle_held, sem):
    fetches, stores = [], []
    whole = ((ladder_in, ladder_held, ladder_out), (cycle_in, cycle_held, cycle_out))
    for n, (source, held, target) in enumerate(whole):
        size = source.shape[0] // PARTS
        for i in range(PARTS):
            sl = pl.ds(i * size, size)
            fetches.append(pltpu.make_async_copy(source.at[sl], held.at[sl], sem.at[0, n, i]))
            stores.append(pltpu.make_async_copy(held.at[sl], target.at[sl], sem.at[1, n, i]))
    for fetch in fetches:
        fetch.start()
    for fetch, store in zip(fetches, stores):
        fetch.wait()
        store.start()
    for store in stores:
        store.wait()


def fused_shards(sizes, amplitudes, factors, cycle_weight, orbital_order):
    groups, rows, cols = sizes
    pairs, one, virtual, _ = amplitudes.shape
    out_width, depth = cycle_weight.shape
    block = virtual // rows
    chunks = block // TILE
    chips = groups * rows // 2
    panel_width = virtual // groups
    span = out_width // PARTS
    half = jnp.bfloat16
    dma = pltpu.SemaphoreType.DMA
    anywhere = pl.BlockSpec(memory_space=pl.ANY)
    matmuls = 2 * out_width * depth * cols * panel_width
    ladder_term, cycle_term = pl.pallas_call(
        functools.partial(kernel, sizes),
        out_shape=(
            jax.ShapeDtypeStruct((pairs, virtual, virtual), half),
            jax.ShapeDtypeStruct((panel_width, out_width), half),
        ),
        in_specs=[pl.BlockSpec(memory_space=pltpu.VMEM), anywhere, anywhere, anywhere],
        out_specs=(anywhere, anywhere),
        scratch_shapes=[
            pltpu.VMEM((chunks, out_width, depth // chunks), half),
            pltpu.VMEM((pairs, virtual, virtual), half),
            pltpu.VMEM((chunks, rows // 2, pairs, TILE, virtual), half),
            pltpu.VMEM((chunks, rows // 2, groups, TILE, 2 * pairs, panel_width), half),
            pltpu.VMEM((cols, chunks, TILE, 2 * pairs * chips, panel_width), half),
            pltpu.VMEM((cols, out_width, panel_width), jnp.float32),
            pltpu.VMEM((rows // 2, out_width, panel_width), half),
            pltpu.VMEM((rows // 2, out_width, panel_width), half),
            pltpu.VMEM((out_width, panel_width), half),
            pltpu.VMEM((out_width, panel_width), half),
            pltpu.VMEM((PARTS, panel_width, span), half),
            pltpu.VMEM((cols, virtual, virtual), half),
            dma((2,)),
            dma((chunks,)),
            dma((chunks, rows // 2)),
            dma((chunks, rows // 2)),
            dma((chunks, chips)),
            dma((chunks, chips)),
            dma((cols, chunks, chips)),
            dma((cols, chunks, chips)),
            dma((cols, chunks, chips)),
            dma((cols - 1,)),
            dma((cols - 1,)),
            dma((groups * rows - 1,)),
            dma((groups * rows - 1,)),
            dma((rows // 2, PARTS)),
            dma((rows // 2, PARTS)),
            dma((PARTS,)),
            dma((PARTS,)),
            dma((PARTS,)),
        ],
        compiler_params=pltpu.CompilerParams(
            collective_id=0, has_side_effects=True, vmem_limit_bytes=60 * 1024 * 1024
        ),
        cost_estimate=pl.CostEstimate(
            flops=matmuls, bytes_accessed=2 * out_width * depth, transcendentals=0
        ),
    )(
        orbital_order.reshape(1, virtual),
        amplitudes.reshape(pairs, virtual, virtual),
        factors,
        cycle_weight,
    )
    ladder_term, cycle_term = pl.pallas_call(
        hand_over,
        out_shape=(
            jax.ShapeDtypeStruct(ladder_term.shape, half),
            jax.ShapeDtypeStruct(cycle_term.shape, half),
        ),
        in_specs=[anywhere, anywhere],
        out_specs=(anywhere, anywhere),
        scratch_shapes=[
            pltpu.VMEM(ladder_term.shape, half),
            pltpu.VMEM(cycle_term.shape, half),
            dma((2, 2, PARTS)),
        ],
        compiler_params=pltpu.CompilerParams(vmem_limit_bytes=60 * 1024 * 1024),
    )(ladder_term, cycle_term)
    return ladder_term.reshape(pairs, one, virtual, virtual), cycle_term


def shards(amplitudes, factors, cycle_weight, orbital_order):
    groups, rows, cols = (lax.axis_size(name) for name in ("grp", "row", "col"))
    pairs, per_col, virtual, _ = amplitudes.shape
    out_width, depth = cycle_weight.shape
    fits = (
        per_col == 1
        and factors.shape[0] == 1
        and rows == cols
        and rows // 2 == 2
        and rows % 2 == 0
        and 2 * pairs == TILE
        and TILE % (groups * rows // 2) == 0
        and virtual == groups * LANES
        and virtual % (rows * TILE) == 0
        and pairs % (virtual // (rows * TILE)) == 0
        and virtual // (rows * TILE) > 1
        and virtual % (groups * rows * TILE) == 0
        and depth == virtual // rows * groups * rows * pairs
        and out_width % (PARTS * LANES) == 0
        and 2 * out_width * depth <= 36 * 1024 * 1024
    )
    if fits:
        return fused_shards((groups, rows, cols), amplitudes, factors, cycle_weight, orbital_order)
    return plain_shards(amplitudes, factors, cycle_weight, orbital_order)


def solution(mesh):
    return jax.shard_map(
        shards,
        mesh=mesh,
        in_specs=(P(("grp", "row"), "col", None, None), P("col", None, None), P("col", "row"), P()),
        out_specs=(P(("grp", "row"), "col", None, None), P(("grp", "row"), "col")),
        check_vma=False,
    )
```

```python
import functools

import jax
import jax.numpy as jnp
from jax import lax
from jax.experimental import pallas as pl
from jax.experimental.pallas import tpu as pltpu
from jax.sharding import PartitionSpec as P

MESH = pl.DeviceIdType.MESH
TILE = 16
LANES = 128
PARTS = 4
NT = (((1,), (1,)), ((), ()))


def dress_pairs(factor_piece, pair_stack):
    dressed = jnp.einsum(
        "pac,qcd->pqad", factor_piece, pair_stack, preferred_element_type=jnp.float32
    ).astype(jnp.bfloat16)
    return jnp.einsum("pqad,pbd->qab", dressed, factor_piece, preferred_element_type=jnp.float32)


def plain_shards(amplitudes, factors, cycle_weight, orbital_order):
    occ_rows = amplitudes.shape[0]
    occ_cols = amplitudes.shape[1]
    virtual = amplitudes.shape[2]
    pair_stack = amplitudes.reshape(occ_rows * occ_cols, virtual, virtual)
    ladder_sum = dress_pairs(lax.all_gather(factors, "col", axis=0, tiled=True), pair_stack)
    ladder_sum = ladder_sum.reshape(occ_rows, occ_cols, virtual, virtual)
    ladder_term = ladder_sum.astype(jnp.bfloat16)
    groups = lax.axis_size("grp")
    row_count = lax.axis_size("row")
    panel_width = virtual // groups
    block_width = virtual // row_count
    ordered = jnp.take(amplitudes, orbital_order, axis=3)
    ordered = ordered.reshape(occ_rows, occ_cols, row_count, block_width, groups, panel_width)
    outgoing = jnp.transpose(ordered, (4, 2, 3, 0, 1, 5))
    outgoing = outgoing.reshape(groups * row_count, block_width, 1, occ_rows, occ_cols, panel_width)
    arrived = lax.all_to_all(outgoing, ("grp", "row"), split_axis=0, concat_axis=2, tiled=True)
    column_tile = arrived.reshape(
        block_width * groups * row_count * occ_rows, occ_cols * panel_width
    )
    products = lax.dot_general(
        lax.all_gather(column_tile, "col", axis=1, tiled=True),
        cycle_weight,
        (((0,), (1,)), ((), ())),
        preferred_element_type=jnp.float32,
    )
    cycle_term = lax.psum_scatter(products, "row", scatter_dimension=0, tiled=True).astype(
        jnp.bfloat16
    )
    return (ladder_term, cycle_term)


def kernel(
    sizes, order_ref, amp, fac, weight, ladder_out, cycle_out,
    wv, own, other, staged, panel, acc, pair_out, pair_in, far_out, far_in, result, fitted,
    load_sem, weight_sem, raw_send, raw_recv, ex_send, ex_recv, up_send, down_send, z_recv,
    fit_send, fit_recv, fan_send, fan_recv, pair_send, pair_recv, far_send, far_recv, out_sem,
):
    groups, rows, cols = sizes
    sides = rows // 2
    chips = groups * sides
    pairs, virtual, _ = amp.shape
    block = virtual // rows
    chunks = block // TILE
    depth = weight.shape[1] // chunks
    span = weight.shape[0] // PARTS
    panel_width = virtual // groups
    g, r, z = lax.axis_index("grp"), lax.axis_index("row"), lax.axis_index("col")
    side, core = r // 2, r % 2
    mate = side * 2 + 1 - core
    chip = g * sides + side
    place = g * rows + r
    fit_rows = virtual // (groups * rows)

    def at(gg, rr, zz):
        return {"grp": gg, "row": rr, "col": zz}

    def remote(src, dst, send, recv, where):
        return pltpu.make_async_remote_copy(
            src_ref=src, dst_ref=dst, send_sem=send, recv_sem=recv,
            device_id=where, device_id_type=MESH,
        )

    mine = pl.ds(pl.multiple_of(place * fit_rows, fit_rows), fit_rows)
    load_own = pltpu.make_async_copy(amp, own, load_sem.at[0])
    load_own.start()
    load_fit = pltpu.make_async_copy(fac.at[0, mine], fitted.at[z, mine], load_sem.at[1])
    load_fit.start()

    def load_weight(c):
        return pltpu.make_async_copy(
            weight.at[:, pl.ds(c * depth, depth)], wv.at[c], weight_sem.at[c]
        )

    for c in range(chunks):
        load_weight(c).start()

    peers = groups * rows - 1
    barrier = pltpu.get_barrier_semaphore()
    for step in range(1, peers + 1):
        q = lax.rem(place + step, groups * rows)
        pl.semaphore_signal(barrier, inc=1, device_id=at(q // rows, q % rows, z), device_id_type=MESH)
    for step in range(1, cols):
        pl.semaphore_signal(
            barrier, inc=1, device_id=at(g, r, lax.rem(z + step, cols)), device_id_type=MESH
        )
    pl.semaphore_wait(barrier, peers + cols - 1)

    def raw_copy(c, s):
        first = pl.multiple_of((s * 2 + 1 - core) * block + c * TILE, TILE)
        return remote(
            amp.at[:, pl.ds(first, TILE)], other.at[c, s], raw_send.at[c, s], raw_recv.at[c, s],
            at(g, mate, z),
        )

    for c in range(chunks):
        for s in range(sides):
            raw_copy(c, s).start()

    load_fit.wait()

    def fit_copy(step):
        here = fitted.at[z, mine]
        return remote(
            here, here, fit_send.at[step - 1], fit_recv.at[step - 1],
            at(g, r, lax.rem(z + step, cols)),
        )

    for step in range(1, cols):
        fit_copy(step).start()

    load_own.wait()

    width = 2 * pairs * TILE
    pick = (
        lax.broadcasted_iota(jnp.int32, (virtual, virtual), 0) == order_ref[...]
    ).astype(jnp.float32).astype(jnp.bfloat16)
    to_row = lax.broadcasted_iota(jnp.int32, (width, width), 0)
    from_row = lax.broadcasted_iota(jnp.int32, (width, width), 1)
    k_row = to_row & (2 * pairs - 1)
    c_row = to_row // (2 * pairs)
    late = (k_row // pairs) ^ core
    turn = (
        from_row == late * (pairs * TILE) + (k_row & (pairs - 1)) * TILE + c_row
    ).astype(jnp.float32).astype(jnp.bfloat16)

    slot = pl.ds(pl.multiple_of(chip * TILE, TILE), TILE)

    def ex_copy(c, s, q):
        return remote(
            staged.at[c, s, q], panel.at[z, c, :, slot, :],
            ex_send.at[c, s * groups + q], ex_recv.at[c, chip], at(q, s * 2 + core, z),
        )

    end_plane = (z == 0) | (z == cols - 1)
    late_block = jnp.where(z == 0, 1, cols - 2)
    late_in = end_plane & (late_block // 2 == side)
    late_up = (z == cols - 2) & ((cols - 2) // 2 == side)
    late_down = (z == 1) & (1 // 2 == side)
    half = chunks // 2

    fine = TILE // chips

    def piece_of(j, c, f, striped):
        if striped:
            return panel.at[j, c, :, pl.ds(pl.multiple_of(f * TILE, TILE), TILE), :]
        return panel.at[j, c, pl.ds(f * fine, fine)]

    def up_copy(j, c, f, striped):
        piece = piece_of(j, c, f, striped)
        return remote(piece, piece, up_send.at[j, c, f], z_recv.at[j, c, f], at(g, r, z + 1))

    def down_copy(j, c, f, striped):
        piece = piece_of(j, c, f, striped)
        return remote(piece, piece, down_send.at[j, c, f], z_recv.at[j, c, f], at(g, r, z - 1))

    def for_pieces(c, act):
        @pl.when(c == 0)
        def _():
            for i in range(chips):
                act(lax.rem(chip + i, chips), True)

        @pl.when(c > 0)
        def _():
            for f in range(chips):
                act(f, False)

    def arrived(c, q):
        @pl.when(q != chip)
        def _():
            landing = piece_of(z, c, q, True)
            remote(
                landing, landing, ex_send.at[c, 0], ex_recv.at[c, q], at(g, mate, z)
            ).wait_recv()

    def send_piece(c, f, striped):
        @pl.when((z + 1 < cols) & jnp.logical_not(late_up & (c >= half)))
        def _():
            up_copy(z, c, f, striped).start()

        @pl.when((z > 0) & jnp.logical_not(late_down & (c >= half)))
        def _():
            down_copy(z, c, f, striped).start()

    def send_own(c):
        @pl.when(c == 0)
        def _():
            for i in range(1, chips):
                q = lax.rem(chip + i, chips)
                arrived(0, q)
                send_piece(0, q, True)

        @pl.when(c > 0)
        def _():
            for q in range(chips):
                arrived(c, q)
            for f in range(chips):
                send_piece(c, f, False)

    def exchange(c, carry):
        for s in range(sides):
            raw_copy(c, s).wait_recv()
        for s in range(sides):
            first = pl.multiple_of((s * 2 + core) * block + c * TILE, TILE)
            near = own[:, pl.ds(first, TILE), :].reshape(pairs * TILE, virtual)
            far = other[c, s].reshape(pairs * TILE, virtual)
            both = jnp.concatenate([near, far], axis=0)
            picked = jnp.dot(both, pick, preferred_element_type=jnp.float32).astype(jnp.bfloat16)
            turned = jnp.dot(turn, picked, preferred_element_type=jnp.float32).astype(jnp.bfloat16)
            for q in range(groups):
                part = turned[:, q * panel_width:(q + 1) * panel_width]
                part = part.reshape(TILE, 2 * pairs, panel_width)
                here = (q == g) & (s == side)

                @pl.when(here)
                def _():
                    panel[z, c, :, slot, :] = part

                @pl.when(jnp.logical_not(here))
                def _():
                    staged[c, s, q] = part
                    ex_copy(c, s, q).start()

        @pl.when(c == 0)
        def _():
            send_piece(0, chip, True)

        @pl.when(c > 0)
        def _():
            send_own(c - 1)

        return carry

    lax.fori_loop(0, chunks, exchange, 0)
    send_own(jnp.int32(chunks - 1))

    def multiply(blocks, c, f=None):
        if f is None:
            wide, start, last = depth, 0, True
            held = [panel[j, c].reshape(depth, panel_width) for j in blocks]
        else:
            wide, last = depth // chips, f == chips - 1
            start = pl.multiple_of(f * wide, wide)
            held = [panel[j, c, pl.ds(f * fine, fine)].reshape(wide, panel_width) for j in blocks]
        piece = jnp.concatenate(held, axis=1)

        def one(i, carry):
            sl = pl.ds(pl.multiple_of(i * span, span), span)
            product = jnp.dot(
                wv[c, sl, pl.ds(start, wide)], piece, preferred_element_type=jnp.float32
            )
            for n, j in enumerate(blocks):
                part = product[:, n * panel_width:(n + 1) * panel_width]

                @pl.when(c == 0)
                def _():
                    acc[j, sl, :] = part

                @pl.when(c > 0)
                def _():
                    acc[j, sl, :] += part

                @pl.when((c == chunks - 1) & last & (j % 2 != core))
                def _():
                    pair_out[j // 2, sl, :] = acc[j, sl, :].astype(jnp.bfloat16)
                    pair_copy(j, i).start()

            return carry

        lax.fori_loop(0, PARTS, one, 0)

    def pair_copy(j, i):
        sl = pl.ds(pl.multiple_of(i * span, span), span)
        h = j // 2
        return remote(
            pair_out.at[h, sl], pair_in.at[h, sl], pair_send.at[h, i], pair_recv.at[h, i],
            at(g, mate, z),
        )

    def far_copy(i):
        sl = pl.ds(pl.multiple_of(i * span, span), span)
        return remote(
            far_out.at[sl], far_in.at[sl], far_send.at[i], far_recv.at[i],
            at(g, (1 - side) * 2 + core, z),
        )

    def pass_on(j):
        @pl.when((j % 2 == core) & (j // 2 != side))
        def _():
            def one(i, carry):
                sl = pl.ds(pl.multiple_of(i * span, span), span)
                pair_copy(j, i).wait_recv()
                total = acc[j, sl, :] + pair_in[j // 2, sl, :].astype(jnp.float32)
                far_out[sl, :] = total.astype(jnp.bfloat16)
                far_copy(i).start()
                return carry

            lax.fori_loop(0, PARTS, one, 0)

    def fan_copy(step):
        q = lax.rem(place + step, groups * rows)
        here = fitted.at[:, mine]
        return remote(
            here, here, fan_send.at[step - 1], fan_recv.at[step - 1], at(q // rows, q % rows, z)
        )

    for step in range(1, cols):
        fit_copy(step).wait_recv()
    for step in range(1, peers + 1):
        fan_copy(step).start()

    def ladder(k):
        left = own[k]
        total = jnp.zeros((virtual, virtual), jnp.float32)
        for p in range(cols):
            dressed = jnp.dot(fitted[p], left, preferred_element_type=jnp.float32)
            total += lax.dot_general(
                dressed.astype(jnp.bfloat16), fitted[p], NT, preferred_element_type=jnp.float32
            )
        own[k] = total.astype(jnp.bfloat16)

    natural = end_plane & jnp.logical_not(late_in)
    before_last = jnp.where(z == 0, cols - 2, 1)
    own_hop = jnp.where(natural, 1, cols - 2)
    ladder_hop = jnp.where(late_in, 1, own_hop + 1)
    per_step = pairs // chunks

    def await_piece(j, c, f):
        piece = piece_of(j, c, f, False)
        remote(piece, piece, up_send.at[j, c, f], z_recv.at[j, c, f], at(g, mate, z)).wait_recv()

    def finish(blocks):
        c = jnp.int32(chunks - 1)

        def one(f, carry):
            await_piece(blocks[-1], c, f)
            multiply(blocks, c, f)
            return carry

        lax.fori_loop(0, chips, one, 0)

    def hop(n, carry):
        low, high = z - n, z + n

        def step(c, inner):
            on_time = jnp.logical_not(late_in & (n == 1) & (c >= half))
            has_low, has_high = (low >= 0) & on_time, (high < cols) & on_time

            ending = end_plane & (n == cols - 1) & (c == chunks - 1) & jnp.logical_not(late_in)

            @pl.when(has_low & jnp.logical_not(ending))
            def _():
                def act(f, striped):
                    up_copy(low, c, f, striped).wait_recv()

                    @pl.when(z + 1 < cols)
                    def _():
                        up_copy(low, c, f, striped).start()

                for_pieces(c, act)

            @pl.when(has_high & jnp.logical_not(ending))
            def _():
                def act(f, striped):
                    down_copy(high, c, f, striped).wait_recv()

                    @pl.when(z > 0)
                    def _():
                        down_copy(high, c, f, striped).start()

                for_pieces(c, act)

            @pl.when((n == cols - 2) & (c == chunks - 1))
            def _():
                for late, copy in ((late_up, up_copy), (late_down, down_copy)):
                    @pl.when(late)
                    def _():
                        for d in range(half, chunks):
                            for f in range(chips):
                                copy(z, d, f, False).start()

            @pl.when(n == 1)
            def _():
                load_weight(c).wait()

            inside = (n == 1) & jnp.logical_not(end_plane)
            other = jnp.where(low >= 0, low, high)

            closing = end_plane & (n == cols - 1)
            beside = jnp.where(late_in, late_block, before_last)
            one_only = closing & late_in & (c >= half)
            first = jnp.where(inside, low, jnp.where(closing, beside, z))

            @pl.when(
                inside | (n == own_hop) | (closing & jnp.logical_not(one_only | ending))
            )
            def _():
                multiply((first, jnp.where(inside, high, other)), c)

            @pl.when(one_only)
            def _():
                multiply((other,), c)

            @pl.when(ending)
            def _():
                finish((before_last, other))

            @pl.when(n == ladder_hop)
            def _():
                @pl.when(c == 0)
                def _():
                    for step in range(1, peers + 1):
                        fan_copy(step).wait_recv()

                for k in range(per_step):
                    ladder(c * per_step + k)

            return inner

        lax.fori_loop(0, chunks, step, 0)
        inside = (n == 1) & jnp.logical_not(end_plane)
        closing = end_plane & (n == cols - 1)
        other = jnp.where(low >= 0, low, high)
        done = (
            (low, inside),
            (high, inside),
            (z, n == own_hop),
            (other, (n == own_hop) | closing),
            (before_last, closing & natural),
        )
        for j, valid in done:
            @pl.when(valid)
            def _():
                pass_on(j)

        @pl.when(n == ladder_hop)
        def _():
            pltpu.make_async_copy(own, ladder_out, load_sem.at[0]).start()

        return carry

    lax.fori_loop(1, cols, hop, 0)

    @pl.when(late_in)
    def _():
        def step(c, carry):
            for f in range(chips):
                await_piece(late_block, c, f)
            multiply((late_block,), c)
            return carry

        lax.fori_loop(half, chunks - 1, step, 0)
        finish((late_block,))

    def out_copy(i):
        return pltpu.make_async_copy(
            result.at[i], cycle_out.at[:, pl.ds(i * span, span)], out_sem.at[i]
        )

    for i in range(PARTS):
        sl = pl.ds(i * span, span)
        pair_copy(r, i).wait_recv()
        far_copy(i).wait_recv()
        total = acc[r, sl, :] + pair_in[side, sl, :].astype(jnp.float32)
        total += far_in[sl, :].astype(jnp.float32)
        result[i] = total.astype(jnp.bfloat16).T
        out_copy(i).start()

    pltpu.make_async_copy(own, ladder_out, load_sem.at[0]).wait()
    for step in range(1, cols):
        fit_copy(step).wait_send()
    for step in range(1, peers + 1):
        fan_copy(step).wait_send()

    def drain(c, carry):
        for s in range(sides):
            raw_copy(c, s).wait_send()
            for q in range(groups):
                @pl.when(jnp.logical_not((q == g) & (s == side)))
                def _():
                    ex_copy(c, s, q).wait_send()
        for j in range(cols):
            @pl.when((j <= z) & (z + 1 < cols))
            def _():
                for_pieces(c, lambda f, striped: up_copy(j, c, f, striped).wait_send())

            @pl.when((j >= z) & (z > 0))
            def _():
                for_pieces(c, lambda f, striped: down_copy(j, c, f, striped).wait_send())
        return carry

    lax.fori_loop(0, chunks, drain, 0)
    for i in range(PARTS):
        for h in range(sides):
            pair_copy(2 * h, i).wait_send()
        far_copy(i).wait_send()
        out_copy(i).wait()


def hand_over(ladder_in, cycle_in, ladder_out, cycle_out, ladder_held, cycle_held, sem):
    fetches, stores = [], []
    whole = ((ladder_in, ladder_held, ladder_out), (cycle_in, cycle_held, cycle_out))
    for n, (source, held, target) in enumerate(whole):
        size = source.shape[0] // PARTS
        for i in range(PARTS):
            sl = pl.ds(i * size, size)
            fetches.append(pltpu.make_async_copy(source.at[sl], held.at[sl], sem.at[0, n, i]))
            stores.append(pltpu.make_async_copy(held.at[sl], target.at[sl], sem.at[1, n, i]))
    for fetch in fetches:
        fetch.start()
    for fetch, store in zip(fetches, stores):
        fetch.wait()
        store.start()
    for store in stores:
        store.wait()


def fused_shards(sizes, amplitudes, factors, cycle_weight, orbital_order):
    groups, rows, cols = sizes
    pairs, one, virtual, _ = amplitudes.shape
    out_width, depth = cycle_weight.shape
    block = virtual // rows
    chunks = block // TILE
    chips = groups * rows // 2
    panel_width = virtual // groups
    span = out_width // PARTS
    half = jnp.bfloat16
    dma = pltpu.SemaphoreType.DMA
    anywhere = pl.BlockSpec(memory_space=pl.ANY)
    matmuls = 2 * out_width * depth * cols * panel_width
    ladder_term, cycle_term = pl.pallas_call(
        functools.partial(kernel, sizes),
        out_shape=(
            jax.ShapeDtypeStruct((pairs, virtual, virtual), half),
            jax.ShapeDtypeStruct((panel_width, out_width), half),
        ),
        in_specs=[pl.BlockSpec(memory_space=pltpu.VMEM), anywhere, anywhere, anywhere],
        out_specs=(anywhere, anywhere),
        scratch_shapes=[
            pltpu.VMEM((chunks, out_width, depth // chunks), half),
            pltpu.VMEM((pairs, virtual, virtual), half),
            pltpu.VMEM((chunks, rows // 2, pairs, TILE, virtual), half),
            pltpu.VMEM((chunks, rows // 2, groups, TILE, 2 * pairs, panel_width), half),
            pltpu.VMEM((cols, chunks, TILE, 2 * pairs * chips, panel_width), half),
            pltpu.VMEM((cols, out_width, panel_width), jnp.float32),
            pltpu.VMEM((rows // 2, out_width, panel_width), half),
            pltpu.VMEM((rows // 2, out_width, panel_width), half),
            pltpu.VMEM((out_width, panel_width), half),
            pltpu.VMEM((out_width, panel_width), half),
            pltpu.VMEM((PARTS, panel_width, span), half),
            pltpu.VMEM((cols, virtual, virtual), half),
            dma((2,)),
            dma((chunks,)),
            dma((chunks, rows // 2)),
            dma((chunks, rows // 2)),
            dma((chunks, chips)),
            dma((chunks, chips)),
            dma((cols, chunks, chips)),
            dma((cols, chunks, chips)),
            dma((cols, chunks, chips)),
            dma((cols - 1,)),
            dma((cols - 1,)),
            dma((groups * rows - 1,)),
            dma((groups * rows - 1,)),
            dma((rows // 2, PARTS)),
            dma((rows // 2, PARTS)),
            dma((PARTS,)),
            dma((PARTS,)),
            dma((PARTS,)),
        ],
        compiler_params=pltpu.CompilerParams(
            collective_id=0, has_side_effects=True, vmem_limit_bytes=60 * 1024 * 1024
        ),
        cost_estimate=pl.CostEstimate(
            flops=matmuls, bytes_accessed=2 * out_width * depth, transcendentals=0
        ),
    )(
        orbital_order.reshape(1, virtual),
        amplitudes.reshape(pairs, virtual, virtual),
        factors,
        cycle_weight,
    )
    ladder_term, cycle_term = pl.pallas_call(
        hand_over,
        out_shape=(
            jax.ShapeDtypeStruct(ladder_term.shape, half),
            jax.ShapeDtypeStruct(cycle_term.shape, half),
        ),
        in_specs=[anywhere, anywhere],
        out_specs=(anywhere, anywhere),
        scratch_shapes=[
            pltpu.VMEM(ladder_term.shape, half),
            pltpu.VMEM(cycle_term.shape, half),
            dma((2, 2, PARTS)),
        ],
        compiler_params=pltpu.CompilerParams(vmem_limit_bytes=60 * 1024 * 1024),
    )(ladder_term, cycle_term)
    return ladder_term.reshape(pairs, one, virtual, virtual), cycle_term


def shards(amplitudes, factors, cycle_weight, orbital_order):
    groups, rows, cols = (lax.axis_size(name) for name in ("grp", "row", "col"))
    pairs, per_col, virtual, _ = amplitudes.shape
    out_width, depth = cycle_weight.shape
    fits = (
        per_col == 1
        and factors.shape[0] == 1
        and rows == cols
        and rows // 2 == 2
        and rows % 2 == 0
        and 2 * pairs == TILE
        and TILE % (groups * rows // 2) == 0
        and virtual == groups * LANES
        and virtual % (rows * TILE) == 0
        and pairs % (virtual // (rows * TILE)) == 0
        and virtual // (rows * TILE) > 1
        and virtual % (groups * rows * TILE) == 0
        and depth == virtual // rows * groups * rows * pairs
        and out_width % (PARTS * LANES) == 0
        and 2 * out_width * depth <= 36 * 1024 * 1024
    )
    if fits:
        return fused_shards((groups, rows, cols), amplitudes, factors, cycle_weight, orbital_order)
    return plain_shards(amplitudes, factors, cycle_weight, orbital_order)


def solution(mesh):
    return jax.shard_map(
        shards,
        mesh=mesh,
        in_specs=(P(("grp", "row"), "col", None, None), P("col", None, None), P("col", "row"), P()),
        out_specs=(P(("grp", "row"), "col", None, None), P(("grp", "row"), "col")),
        check_vma=False,
    )
```
